128 devices in a mesh: dp: 16 (over z, x), seq: 8 (over y, core).
Axes of the slice: x: 4, y: 4, z: 4, core: 2. Of those that a mesh axis runs over, the one named last changes fastest.
Arguments:
- tokens: bfloat16 [98304, 2048], P(('dp', 'seq')), may hold values from -6 to 6
- norm_gain: float32 [2048], replicated, may hold values from 0.5 to 1.5
- qkv_weight: bfloat16 [3, 2048, 1024], replicated, may hold values from -0.125 to 0.125
- beta_weight: bfloat16 [2048, 8], replicated, may hold values from -0.125 to 0.125
- beta_bias: float32 [8], replicated, may hold values from -7 to 1
- out_weight: bfloat16 [1024, 2048], replicated, may hold values from -0.1875 to 0.1875
- doc_lengths: int32 [16, 8], replicated, may hold values from 1 to 3840, 6144 in all within a row
- source_dp: int32 [16, 8, 16], replicated, may hold values from 0 to 15, as said below
- source_offset: int32 [16, 8, 16], replicated, may hold values from 0 to 720, as said below
Outputs:
- mixed: bfloat16 [98304, 2048], P(('dp', 'seq'))
The draws below stay inside these ranges and needn't reach their ends.
Inputs may be any that keep to these rules, and one draw needn't show every extreme that they name: `source_dp`: for each seq index j, the slots of all owners take every piece of 48 rows of every arrival device (p, j) exactly once, and no owner takes two pieces from one arrival device. `source_offset`: A multiple of 48. `doc_lengths`: each row sums to 6144.
All inputs are finite; a program needn't handle non-finite values.
Results may differ from the reference program's by a relative error of at most 0.02.
Values may be sent and summed in bfloat16 or wider, within the bound.
A program may use at most 128 MiB of HBM per device.

```python
import math
import jax
import jax.numpy as jnp
import numpy as np
from jax import lax

D = 2048
H = 8
HEAD = 128
NDOCS = 8
TOK_DEV = 768
TOKENS = 98304
SEQ_TOK = 6144
PIECES = 16
PIECE = 48
LONGEST = 3840
N_DP = 16
N_SEQ = 8


def plan_tables(key):

    def one_index(seq_key):
        key_first, key_second, key_third, key_fourth = jax.random.split(seq_key, 4)
        sender_place = jax.random.permutation(key_first, N_DP)
        sender_at = jnp.argsort(sender_place)
        target_place = jnp.argsort(jax.random.permutation(key_second, N_DP))
        slot_order = jax.vmap(lambda sub_key: jax.random.permutation(sub_key, PIECES))(jax.random.split(key_third, N_DP))
        piece_index = jnp.argsort(slot_order, axis=1)
        piece_order = jax.vmap(lambda sub_key: jax.random.permutation(sub_key, PIECES))(jax.random.split(key_fourth, N_DP))
        sender = sender_at[(target_place[:, None] - piece_index) % N_DP]
        offset = piece_order[sender, piece_index] * PIECE
        return (sender.astype(jnp.int32), offset.astype(jnp.int32))
    senders, offsets = jax.vmap(one_index)(jax.random.split(key, N_SEQ))
    return (jnp.transpose(senders, (1, 0, 2)), jnp.transpose(offsets, (1, 0, 2)))


def draw_source_dp(key, part):
    senders, offsets = plan_tables(key)
    return senders


def draw_source_offset(key, part):
    senders, offsets = plan_tables(key)
    return offsets


def steps_of(rng, shape, shards, low, largest):
    def one(axis_at, parts):
        steps = jax.random.uniform(jax.random.fold_in(jax.random.fold_in(rng, 6), axis_at), (parts,), jnp.float32, low / len(shards), largest / len(shards))
        return jnp.repeat(jnp.exp(steps), shape[axis_at] // parts).reshape((-1,) + (1,) * (len(shape) - axis_at - 1))

    gain = one(*shards[0])
    for cut in shards[1:]:
        gain = gain * one(*cut)
    return gain


def length_profile(count, total, reach, skew):
    weights = [(1 << 20) // math.isqrt(rank ** skew) + 1 for rank in range(2, count + 1)]
    rest, holding = total - reach - (count - 1), [1] * (count - 1)
    while rest > 0:
        free = [i for i in range(count - 1) if holding[i] < reach]
        pool, budget = sum([weights[i] for i in free]), rest
        for i in free:
            addition = min(reach - holding[i], max(1, budget * weights[i] // pool), rest)
            holding[i] = holding[i] + addition
            rest = rest - addition
    return np.array([reach] + holding)


def ragged_sizes(stream_key, count, total, bound, skew):
    if count == 2:
        one = jax.random.randint(stream_key, (), max(1, total - bound), min(bound, total - 1) + 1)
        return jnp.stack([one, total - one])
    lengths = jnp.asarray(length_profile(count, total, bound, skew), jnp.int32)
    pairs = (count - 1) // 2
    donor, taker = lengths[1:1 + 2 * pairs:2], lengths[2:2 + 2 * pairs:2]
    room = jnp.minimum(donor - 1, bound - taker)
    shifted = jax.random.randint(jax.random.fold_in(stream_key, 1), (pairs,), 0, 1 << 20) % (room + 1)
    lengths = lengths.at[1:1 + 2 * pairs:2].set(donor - shifted).at[2:2 + 2 * pairs:2].set(taker + shifted)
    return lengths[jax.random.permutation(jax.random.fold_in(stream_key, 2), count)]


def scatter_about(stream_key, shape, scale, most, pieces=(), kind=jnp.bfloat16):
    drawn = jax.random.normal(stream_key, shape, jnp.float32) * scale
    if len(pieces) > 0:
        drawn = steps_of(stream_key, shape, pieces, -0.22, 0.18) * drawn
    return jnp.clip(drawn, min=-most, max=most).astype(kind)


def setup_inputs(seed: int = 0) -> dict:
    key_list = jax.random.split(jax.random.key(seed), 10)
    return {
        "tokens": scatter_about(key_list[0], (TOKENS, D), 1.0, 6.0, ((0, 128),)),
        "norm_gain": jnp.clip(1.0 + 0.1 * jax.random.normal(key_list[1], (D,), jnp.float32), 0.5, 1.5),
        "qkv_weight": scatter_about(key_list[2], (3, D, H * HEAD), D ** -0.5, 0.125),
        "beta_weight": scatter_about(key_list[3], (D, H), D ** -0.5, 0.125),
        "beta_bias": jnp.clip(jax.random.uniform(key_list[4], (H,), jnp.float32, -7.0, 1.0), -7.0, 1.0),
        "out_weight": scatter_about(key_list[5], (H * HEAD, D), (H * HEAD) ** -0.5, 0.1875),
        "doc_lengths": jax.vmap(lambda own: ragged_sizes(own, NDOCS, SEQ_TOK, LONGEST, 2))(jax.random.split(key_list[6], N_DP)).reshape((N_DP, NDOCS)).astype(jnp.int32),
        "source_dp": draw_source_dp(jax.random.fold_in(key_list[9], 71), 0),
        "source_offset": draw_source_offset(jax.random.fold_in(key_list[9], 71), 0),
    }


rms_epsilon = 1e-06

def reference(tokens, norm_gain, qkv_weight, beta_weight, beta_bias, out_weight, doc_lengths, source_dp, source_offset):
    seq_tokens = N_SEQ * TOK_DEV
    seq_place = jnp.arange(N_SEQ, dtype=jnp.int32)[None, :, None, None]
    within = jnp.arange(PIECE, dtype=jnp.int32)[None, None, None, :]
    arrival = ((source_dp[..., None] * N_SEQ + seq_place) * TOK_DEV + source_offset[..., None] + within).reshape(-1).astype(jnp.int32)
    owned = jnp.take(tokens, arrival, axis=0)
    rows_float = owned.astype(jnp.float32)
    normed = (rows_float * lax.rsqrt(lax.optimization_barrier(jnp.mean(rows_float * rows_float, axis=1, keepdims=True)) + rms_epsilon) * norm_gain).astype(jnp.bfloat16)
    query_rows = jnp.dot(normed, qkv_weight[0], preferred_element_type=jnp.float32).astype(jnp.bfloat16)
    key_rows = jnp.dot(normed, qkv_weight[1], preferred_element_type=jnp.float32).astype(jnp.bfloat16)
    value_rows = jnp.dot(normed, qkv_weight[2], preferred_element_type=jnp.float32).astype(jnp.bfloat16)
    strength = jax.nn.sigmoid(jnp.dot(normed, beta_weight, preferred_element_type=jnp.float32) + beta_bias)
    query_float = query_rows.astype(jnp.float32).reshape(N_DP, seq_tokens, H, HEAD)
    key_float = key_rows.astype(jnp.float32).reshape(N_DP, seq_tokens, H, HEAD)
    value_float = value_rows.astype(jnp.float32).reshape(N_DP, seq_tokens, H, HEAD)
    strength = strength.reshape(N_DP, seq_tokens, H)
    step_size = strength / (1.0 + strength * lax.optimization_barrier(jnp.sum(key_float * key_float, axis=3)))
    starts = jnp.cumsum(doc_lengths, axis=1) - doc_lengths
    position = jnp.arange(seq_tokens, dtype=jnp.int32)
    no_reset = 1.0 - jnp.any(starts[:, None, :] == position[None, :, None], axis=2).astype(jnp.float32)

    def advance(state_now, inputs):
        query_now, key_now, value_now, step_now, keep_now = inputs
        decay_now = 1.0 - step_now[:, :, None] * key_now * key_now
        state_next = state_now * (keep_now[:, None, None, None] * decay_now[:, :, None, :])
        state_next = state_next + (step_now[:, :, None] * value_now)[:, :, :, None] * key_now[:, :, None, :]
        return (state_next, jnp.einsum('bhij,bhj->bhi', state_next, query_now))
    zero_state = jnp.zeros((N_DP, H, HEAD, HEAD), jnp.float32)
    series = (jnp.moveaxis(query_float, 1, 0), jnp.moveaxis(key_float, 1, 0), jnp.moveaxis(value_float, 1, 0), jnp.moveaxis(step_size, 1, 0), jnp.moveaxis(no_reset, 1, 0))
    final_state, outputs = lax.scan(advance, zero_state, series)
    attended = jnp.moveaxis(outputs, 0, 1).reshape(N_DP * seq_tokens, H * HEAD).astype(jnp.bfloat16)
    projected = jnp.dot(attended, out_weight, preferred_element_type=jnp.float32).astype(jnp.bfloat16)
    return jnp.zeros_like(tokens).at[arrival].set(projected)
```

```python
import jax
import jax.numpy as jnp
import numpy as np
from jax import lax
from jax.experimental import pallas as pl
from jax.experimental.pallas import tpu as pltpu
from jax.sharding import PartitionSpec as P

PIECE = 48
SUB = 12


def decay_sums():
    row = np.arange(PIECE)[:, None]
    col = np.arange(PIECE)[None, :]

    def between(low, high):
        return ((col > low) & (col <= high)).astype(np.float32)

    mid = (row // SUB) * SUB + SUB // 2 - 1
    near = between(mid, row) - between(row, mid)
    half = (row // (2 * SUB)) * (2 * SUB) + SUB - 1
    pair = between(half, row) + between(row, half)
    middle = np.full_like(row, 2 * SUB - 1)
    whole = between(middle, row) + between(row, middle)
    before = between(np.full_like(row, -1), row)
    after = between(row, np.full_like(row, PIECE - 1))
    sums = np.concatenate([near, pair, whole, before, after], axis=0)
    return np.concatenate([sums, sums], axis=1)


def dot_nt(a, b):
    return lax.dot_general(a, b, (((1,), (1,)), ((), ())), preferred_element_type=jnp.float32)


def dot_tn(a, b):
    return lax.dot_general(a, b, (((0,), (0,)), ((), ())), preferred_element_type=jnp.float32)


def recurrence_kernel(
    slot_source, starts, place, q_ref, k_ref, v_ref, logit_ref, sums_ref,
    out_ref, carry_ref, state_ref, decay_ref, state, total,
):
    heads = state.shape[0]
    size = state.shape[1]
    state[...] = jnp.zeros_like(state)
    total[...] = jnp.ones_like(total)
    down = lax.broadcasted_iota(jnp.int32, (PIECE, PIECE), 0)
    across = lax.broadcasted_iota(jnp.int32, (PIECE, PIECE), 1)
    wide = lax.broadcasted_iota(jnp.int32, (PIECE, size), 0)
    causal = down >= across
    in_sub = causal & (down // SUB == across // SUB)
    in_pair = causal & (down // (2 * SUB) == across // (2 * SUB)) & (down // SUB != across // SUB)
    in_whole = causal & (down // (2 * SUB) != across // (2 * SUB))
    right_pair = (wide // SUB) % 2 == 1
    right_whole = wide >= 2 * SUB

    def document_of(position):
        count = jnp.zeros_like(position)
        for n in range(starts.shape[0]):
            count = count + (starts[n] <= position).astype(jnp.int32)
        return count

    @pl.loop(0, q_ref.shape[0])
    def _(slot):
        piece = slot_source[slot]
        first = place[0] + slot * PIECE
        doc_down = document_of(first + down)
        doc_across = document_of(first + across)
        doc_wide = document_of(first + wide)
        doc_before = document_of(first - 1)
        doc_last = document_of(first + PIECE - 1)
        same = doc_down == doc_across
        near_mask, pair_mask, whole_mask = in_sub & same, in_pair & same, in_whole & same
        reaches = (doc_wide == doc_before).astype(jnp.float32)
        stays = (doc_wide == doc_last).astype(jnp.float32)
        kept = (doc_last == doc_before).astype(jnp.float32)
        strength = 1.0 / (1.0 + jnp.exp(-logit_ref[piece]))
        rows = pl.ds(pl.multiple_of(slot * PIECE, PIECE), PIECE)
        for h in range(heads):
            cols = slice(h * size, (h + 1) * size)
            query = q_ref[piece, :, cols].astype(jnp.float32)
            key = k_ref[piece, :, cols].astype(jnp.float32)
            value = v_ref[piece, :, cols].astype(jnp.float32)
            squares = key * key
            now = strength[:, h : h + 1]
            step = now / (1.0 + now * jnp.sum(squares, axis=1, keepdims=True))
            log_decay = jnp.log(1.0 - step * squares)
            high = log_decay.astype(jnp.bfloat16)
            low = (log_decay - high.astype(jnp.float32)).astype(jnp.bfloat16)
            gaps = jnp.dot(
                sums_ref[...], jnp.concatenate([high, low], axis=0),
                preferred_element_type=jnp.float32,
            )
            near = gaps[:PIECE]
            pair = gaps[PIECE : 2 * PIECE]
            whole = gaps[2 * PIECE : 3 * PIECE]
            before = gaps[3 * PIECE : 4 * PIECE]
            after = gaps[4 * PIECE :]
            near_query = (query * jnp.exp(near)).astype(jnp.bfloat16)
            near_key = (key * jnp.exp(-near)).astype(jnp.bfloat16)
            pair_both = (jnp.where(right_pair, query, key) * jnp.exp(pair)).astype(jnp.bfloat16)
            whole_both = (jnp.where(right_whole, query, key) * jnp.exp(whole)).astype(jnp.bfloat16)
            scores = jnp.where(
                near_mask,
                dot_nt(near_query, near_key),
                jnp.where(
                    pair_mask,
                    dot_nt(pair_both, pair_both),
                    jnp.where(whole_mask, dot_nt(whole_both, whole_both), 0.0),
                ),
            )
            stepped = value * step
            carried = query * (jnp.exp(before) * reaches)
            now_state = state[h]
            out = jnp.dot(
                scores.astype(jnp.bfloat16), stepped.astype(jnp.bfloat16),
                preferred_element_type=jnp.float32,
            )
            out = out + dot_nt(carried.astype(jnp.bfloat16), now_state.astype(jnp.bfloat16))
            out_ref[rows, cols] = out
            total_now = total[h : h + 1, :]
            carry_ref[rows, cols] = (carried * total_now).astype(jnp.bfloat16)
            decay = jnp.exp(before[PIECE - 1 :, :]) * kept
            total[h : h + 1, :] = total_now * decay
            state[h] = now_state * decay + dot_tn(
                stepped.astype(jnp.bfloat16),
                (key * (jnp.exp(after) * stays)).astype(jnp.bfloat16),
            )

    state_ref[...] = state[...]
    decay_ref[...] = total[...]


def recurrence(slot_source, starts, place, q, k, v, logits):
    pieces, piece_rows, width = q.shape
    heads = logits.shape[2]
    size = width // heads
    sums = jnp.asarray(decay_sums(), jnp.bfloat16)
    smem = pl.BlockSpec(memory_space=pltpu.SMEM)
    vmem = pl.BlockSpec(memory_space=pltpu.VMEM)
    return pl.pallas_call(
        recurrence_kernel,
        out_shape=(
            jax.ShapeDtypeStruct((pieces * piece_rows, width), jnp.float32),
            jax.ShapeDtypeStruct((pieces * piece_rows, width), jnp.bfloat16),
            jax.ShapeDtypeStruct((heads, size, size), jnp.float32),
            jax.ShapeDtypeStruct((heads, size), jnp.float32),
        ),
        in_specs=[smem] * 3 + [vmem] * 5,
        out_specs=[vmem] * 4,
        scratch_shapes=[
            pltpu.VMEM((heads, size, size), jnp.float32),
            pltpu.VMEM((heads, size), jnp.float32),
        ],
        compiler_params=pltpu.CompilerParams(vmem_limit_bytes=40 << 20),
    )(slot_source, starts, place, q, k, v, logits, sums)


rms_epsilon = 1e-06


def shards(
    tokens,
    norm_gain,
    qkv_weight,
    beta_weight,
    beta_bias,
    out_weight,
    doc_lengths,
    source_dp,
    source_offset,
):
    groups = lax.axis_size("dp")
    dp_index = lax.axis_index("dp")
    seq_index = lax.axis_index("seq")
    tok_dev, model_width = tokens.shape
    piece_rows = tok_dev // groups
    head_count = beta_weight.shape[1]
    head_size = qkv_weight.shape[2] // head_count
    plan_source = lax.dynamic_index_in_dim(source_dp, seq_index, 1, keepdims=False)
    plan_offset = lax.dynamic_index_in_dim(source_offset, seq_index, 1, keepdims=False)
    from_here = plan_source == dp_index
    sent_piece = jnp.sum(jnp.where(from_here, plan_offset, 0), axis=1) // piece_rows
    outgoing = tokens.reshape(groups, piece_rows, model_width)[sent_piece]
    incoming = lax.all_to_all(outgoing, "dp", split_axis=0, concat_axis=0, tiled=True)
    slot_source = lax.dynamic_index_in_dim(plan_source, dp_index, 0, keepdims=False)
    owned = incoming.reshape(tok_dev, model_width)
    rows_float = owned.astype(jnp.float32)
    normed = (
        rows_float
        * lax.rsqrt(jnp.mean(rows_float * rows_float, axis=1, keepdims=True) + rms_epsilon)
        * norm_gain
    ).astype(jnp.bfloat16)
    query_rows, key_rows, value_rows = (
        jnp.dot(normed, qkv_weight[n], preferred_element_type=jnp.float32)
        .astype(jnp.bfloat16)
        .reshape(groups, piece_rows, -1)
        for n in range(3)
    )
    logits = jnp.dot(normed, beta_weight, preferred_element_type=jnp.float32) + beta_bias
    logits = logits.reshape(groups, piece_rows, head_count)
    lengths = lax.dynamic_index_in_dim(doc_lengths, dp_index, 0, keepdims=False)
    starts = jnp.cumsum(lengths) - lengths
    place = (seq_index * tok_dev).astype(jnp.int32).reshape(1)
    heads_out, carried, local_state, decay_all = recurrence(
        slot_source, starts, place, query_rows, key_rows, value_rows, logits
    )
    all_decay = lax.all_gather(decay_all, "seq")
    all_state = lax.all_gather(local_state, "seq")
    before = jnp.zeros_like(local_state)
    for k in range(lax.axis_size("seq") - 1):
        before = jnp.where(k < seq_index, before * all_decay[k][:, None, :] + all_state[k], before)
    heads_out = heads_out.reshape(tok_dev, head_count, head_size) + jnp.einsum(
        "thj,hij->thi",
        carried.reshape(tok_dev, head_count, head_size),
        before.astype(jnp.bfloat16),
        preferred_element_type=jnp.float32,
    )
    attended = heads_out.reshape(tok_dev, head_count * head_size).astype(jnp.bfloat16)
    numbers = jnp.arange(groups, dtype=jnp.int32)
    slot_for = jnp.sum(
        jnp.where(slot_source[None, :] == numbers[:, None], numbers[None, :], 0), axis=1
    )
    target_for = jnp.sum(
        jnp.where(sent_piece[None, :] == numbers[:, None], numbers[None, :], 0), axis=1
    )
    returned = lax.all_to_all(
        attended.reshape(groups, piece_rows, -1)[slot_for],
        "dp",
        split_axis=0,
        concat_axis=0,
        tiled=True,
    )
    returned = returned[target_for].reshape(tok_dev, -1)
    return jnp.dot(returned, out_weight, preferred_element_type=jnp.float32).astype(jnp.bfloat16)


def solution(mesh):
    return jax.shard_map(
        shards,
        mesh=mesh,
        in_specs=(P(("dp", "seq"), None), P(), P(), P(), P(), P(), P(), P(), P()),
        out_specs=P(("dp", "seq"), None),
        check_vma=False,
    )
```

```python
import jax
import jax.numpy as jnp
import numpy as np
from jax import lax
from jax.experimental import pallas as pl
from jax.experimental.pallas import tpu as pltpu
from jax.sharding import PartitionSpec as P

MESH = pl.DeviceIdType.MESH
rms_epsilon = 1e-06
ORDER = [(1, 0), (3, 3), (2, 3), (1, 3), (1, 2), (0, 1), (2, 0), (3, 0), (3, 1), (2, 2), (0, 2), (3, 2), (1, 1), (0, 3), (2, 1)]


def peer_along(offset, sign):
    me = lax.axis_index("dp")
    down, right = offset
    row = lax.rem(me // 4 + (down if sign > 0 else 4 - down), 4)
    column = lax.rem(lax.rem(me, 4) + (right if sign > 0 else 4 - right), 4)
    return row * 4 + column


def greet_group(barrier, groups):
    me, seq = lax.axis_index("dp"), lax.axis_index("seq")
    for distance in range(1, groups):
        pl.semaphore_signal(
            barrier, inc=1, device_id=(lax.rem(me + distance, groups), seq), device_id_type=MESH
        )


def arrive_kernel(
    sent, tokens, gain_ref, weight, beta_ref, bias_ref, q_ref, k_ref, v_ref, logit_ref,
    held, send, recv, weight_held, normed, token_sem, weight_sem, send_sem, recv_sem,
):
    groups, piece_rows, model_width = held.shape
    width = q_ref.shape[2]
    me, seq = lax.axis_index("dp"), lax.axis_index("seq")
    token_copy = pltpu.make_async_copy(tokens, held, token_sem)
    token_copy.start()
    weight_copy = pltpu.make_async_copy(weight, weight_held, weight_sem)
    barrier = pltpu.get_barrier_semaphore()
    greet_group(barrier, groups)
    token_copy.wait()
    weight_copy.start()
    recv[me] = held[sent[me]]
    pl.semaphore_wait(barrier, groups - 1)
    copies = []
    for offset in ORDER:
        target = peer_along(offset, 1)
        send[target] = held[sent[target]]
        copy = pltpu.make_async_remote_copy(
            src_ref=send.at[target], dst_ref=recv.at[me], send_sem=send_sem.at[target],
            recv_sem=recv_sem.at[me], device_id=(target, seq), device_id_type=MESH,
        )
        copy.start()
        copies.append(copy)
    weight_copy.wait()
    sources = [me] + [peer_along(offset, -1) for offset in ORDER]
    together = normed.shape[0] // piece_rows
    for first in range(0, groups, together):
        for n in range(together):
            source = sources[first + n]
            if first + n > 0:
                pltpu.make_async_remote_copy(
                    src_ref=send.at[source], dst_ref=recv.at[source], send_sem=send_sem.at[source],
                    recv_sem=recv_sem.at[source], device_id=(source, seq), device_id_type=MESH,
                ).wait_recv()
            rows = recv[source].astype(jnp.float32)
            normed[n * piece_rows : (n + 1) * piece_rows, :] = (
                rows
                * lax.rsqrt(jnp.mean(rows * rows, axis=1, keepdims=True) + rms_epsilon)
                * gain_ref[...]
            ).astype(jnp.bfloat16)
        logits = (
            jnp.dot(normed[...], beta_ref[...], preferred_element_type=jnp.float32) + bias_ref[...]
        )
        for n in range(together):
            logit_ref[sources[first + n]] = logits[n * piece_rows : (n + 1) * piece_rows]
        tile = 512
        for part, target_ref in enumerate((q_ref, k_ref, v_ref)):
            for start in range(0, width, tile):
                cols = slice(start, start + tile)
                product = jnp.dot(
                    normed[...], weight_held[part, :, cols], preferred_element_type=jnp.float32
                ).astype(jnp.bfloat16)
                for n in range(together):
                    target_ref[sources[first + n], :, cols] = product[
                        n * piece_rows : (n + 1) * piece_rows
                    ]
    for copy in copies:
        copy.wait_send()


def arrive(sent, tokens, gain, weight, beta, bias):
    groups = sent.shape[0]
    rows, model_width = tokens.shape
    piece_rows = rows // groups
    width = weight.shape[2]
    heads = beta.shape[1]
    smem = pl.BlockSpec(memory_space=pltpu.SMEM)
    vmem = pl.BlockSpec(memory_space=pltpu.VMEM)
    hbm = pl.BlockSpec(memory_space=pl.ANY)
    part = jax.ShapeDtypeStruct((groups, piece_rows, width), jnp.bfloat16)
    pieces = (groups, piece_rows, model_width)
    return pl.pallas_call(
        arrive_kernel,
        out_shape=(part, part, part, jax.ShapeDtypeStruct((groups, piece_rows, heads), jnp.float32)),
        in_specs=[smem, hbm, vmem, hbm, vmem, vmem],
        out_specs=[vmem] * 4,
        scratch_shapes=[
            pltpu.VMEM(pieces, jnp.bfloat16),
            pltpu.VMEM(pieces, jnp.bfloat16),
            pltpu.VMEM(pieces, jnp.bfloat16),
            pltpu.VMEM(weight.shape, jnp.bfloat16),
            pltpu.VMEM((4 * piece_rows, model_width), jnp.bfloat16),
            pltpu.SemaphoreType.DMA,
            pltpu.SemaphoreType.DMA,
            pltpu.SemaphoreType.DMA((groups,)),
            pltpu.SemaphoreType.DMA((groups,)),
        ],
        compiler_params=pltpu.CompilerParams(
            collective_id=0, has_side_effects=True, vmem_limit_bytes=50 << 20
        ),
    )(sent, tokens.reshape(pieces), gain.reshape(1, -1), weight, beta, bias.reshape(1, -1))


PIECE = 48
SUB = 12


def decay_sums():
    row = np.arange(PIECE)[:, None]
    col = np.arange(PIECE)[None, :]

    def between(low, high):
        return ((col > low) & (col <= high)).astype(np.float32)

    mid = (row // SUB) * SUB + SUB // 2 - 1
    near = between(mid, row) - between(row, mid)
    half = (row // (2 * SUB)) * (2 * SUB) + SUB - 1
    pair = between(half, row) + between(row, half)
    middle = np.full_like(row, 2 * SUB - 1)
    whole = between(middle, row) + between(row, middle)
    before = between(np.full_like(row, -1), row)
    after = between(row, np.full_like(row, PIECE - 1))
    sums = np.concatenate([near, pair, whole, before, after], axis=0)
    return np.concatenate([sums, sums], axis=1)


def dot_nt(a, b):
    return lax.dot_general(a, b, (((1,), (1,)), ((), ())), preferred_element_type=jnp.float32)


def dot_tn(a, b):
    return lax.dot_general(a, b, (((0,), (0,)), ((), ())), preferred_element_type=jnp.float32)


def recurrence_kernel(
    slot_source, starts, place, q_ref, k_ref, v_ref, logit_ref, sums_ref,
    out_ref, carry_ref, state_ref, decay_ref, state, total,
):
    heads = state.shape[0]
    size = state.shape[1]
    state[...] = jnp.zeros_like(state)
    total[...] = jnp.ones_like(total)
    down = lax.broadcasted_iota(jnp.int32, (PIECE, PIECE), 0)
    across = lax.broadcasted_iota(jnp.int32, (PIECE, PIECE), 1)
    wide = lax.broadcasted_iota(jnp.int32, (PIECE, size), 0)
    causal = down >= across
    in_sub = causal & (down // SUB == across // SUB)
    in_pair = causal & (down // (2 * SUB) == across // (2 * SUB)) & (down // SUB != across // SUB)
    in_whole = causal & (down // (2 * SUB) != across // (2 * SUB))
    right_pair = (wide // SUB) % 2 == 1
    right_whole = wide >= 2 * SUB

    def document_of(position):
        count = jnp.zeros_like(position)
        for n in range(starts.shape[0]):
            count = count + (starts[n] <= position).astype(jnp.int32)
        return count

    @pl.loop(0, q_ref.shape[0])
    def _(slot):
        piece = slot_source[slot]
        first = place[0] + slot * PIECE
        doc_down = document_of(first + down)
        doc_across = document_of(first + across)
        doc_wide = document_of(first + wide)
        doc_before = document_of(first - 1)
        doc_last = document_of(first + PIECE - 1)
        same = doc_down == doc_across
        near_mask, pair_mask, whole_mask = in_sub & same, in_pair & same, in_whole & same
        reaches = (doc_wide == doc_before).astype(jnp.float32)
        stays = (doc_wide == doc_last).astype(jnp.float32)
        kept = (doc_last == doc_before).astype(jnp.float32)
        strength = 1.0 / (1.0 + jnp.exp(-logit_ref[piece]))
        rows = pl.ds(pl.multiple_of(slot * PIECE, PIECE), PIECE)
        for h in range(heads):
            cols = slice(h * size, (h + 1) * size)
            query = q_ref[piece, :, cols].astype(jnp.float32)
            key = k_ref[piece, :, cols].astype(jnp.float32)
            value = v_ref[piece, :, cols].astype(jnp.float32)
            squares = key * key
            now = strength[:, h : h + 1]
            step = now / (1.0 + now * jnp.sum(squares, axis=1, keepdims=True))
            log_decay = jnp.log(1.0 - step * squares)
            high = log_decay.astype(jnp.bfloat16)
            low = (log_decay - high.astype(jnp.float32)).astype(jnp.bfloat16)
            gaps = jnp.dot(
                sums_ref[...], jnp.concatenate([high, low], axis=0),
                preferred_element_type=jnp.float32,
            )
            near = gaps[:PIECE]
            pair = gaps[PIECE : 2 * PIECE]
            whole = gaps[2 * PIECE : 3 * PIECE]
            before = gaps[3 * PIECE : 4 * PIECE]
            after = gaps[4 * PIECE :]
            near_query = (query * jnp.exp(near)).astype(jnp.bfloat16)
            near_key = (key * jnp.exp(-near)).astype(jnp.bfloat16)
            pair_both = (jnp.where(right_pair, query, key) * jnp.exp(pair)).astype(jnp.bfloat16)
            whole_both = (jnp.where(right_whole, query, key) * jnp.exp(whole)).astype(jnp.bfloat16)
            scores = jnp.where(
                near_mask,
                dot_nt(near_query, near_key),
                jnp.where(
                    pair_mask,
                    dot_nt(pair_both, pair_both),
                    jnp.where(whole_mask, dot_nt(whole_both, whole_both), 0.0),
                ),
            )
            stepped = value * step
            carried = query * (jnp.exp(before) * reaches)
            now_state = state[h]
            out = jnp.dot(
                scores.astype(jnp.bfloat16), stepped.astype(jnp.bfloat16),
                preferred_element_type=jnp.float32,
            )
            out = out + dot_nt(carried.astype(jnp.bfloat16), now_state.astype(jnp.bfloat16))
            out_ref[rows, cols] = out
            total_now = total[h : h + 1, :]
            carry_ref[rows, cols] = (carried * total_now).astype(jnp.bfloat16)
            decay = jnp.exp(before[PIECE - 1 :, :]) * kept
            total[h : h + 1, :] = total_now * decay
            state[h] = now_state * decay + dot_tn(
                stepped.astype(jnp.bfloat16),
                (key * (jnp.exp(after) * stays)).astype(jnp.bfloat16),
            )

    state_ref[...] = state[...]
    decay_ref[...] = total[...]


def recurrence(slot_source, starts, place, q, k, v, logits):
    pieces, piece_rows, width = q.shape
    heads = logits.shape[2]
    size = width // heads
    sums = jnp.asarray(decay_sums(), jnp.bfloat16)
    smem = pl.BlockSpec(memory_space=pltpu.SMEM)
    vmem = pl.BlockSpec(memory_space=pltpu.VMEM)
    return pl.pallas_call(
        recurrence_kernel,
        out_shape=(
            jax.ShapeDtypeStruct((pieces * piece_rows, width), jnp.float32),
            jax.ShapeDtypeStruct((pieces * piece_rows, width), jnp.bfloat16),
            jax.ShapeDtypeStruct((heads, size, size), jnp.float32),
            jax.ShapeDtypeStruct((heads, size), jnp.float32),
        ),
        in_specs=[smem] * 3 + [vmem] * 5,
        out_specs=[vmem] * 4,
        scratch_shapes=[
            pltpu.VMEM((heads, size, size), jnp.float32),
            pltpu.VMEM((heads, size), jnp.float32),
        ],
        compiler_params=pltpu.CompilerParams(vmem_limit_bytes=40 << 20),
    )(slot_source, starts, place, q, k, v, logits, sums)


def return_kernel(
    slot_for, out_ref, carry_ref, state_ref, decay_ref, weight, result,
    chain_send, chain_recv, send, recv, weight_held, gathered, projected,
    weight_sem, chain_send_sem, chain_recv_sem, send_sem, recv_sem, result_sem,
):
    groups, piece_rows, width = send.shape
    heads, size, _ = state_ref.shape
    me, seq = lax.axis_index("dp"), lax.axis_index("seq")
    peers = lax.axis_size("seq")
    following, previous = lax.rem(seq + 1, peers), lax.rem(seq + peers - 1, peers)
    weight_copy = pltpu.make_async_copy(weight, weight_held, weight_sem)
    weight_copy.start()
    barrier = pltpu.get_barrier_semaphore()
    greet_group(barrier, groups)
    pl.semaphore_signal(barrier, inc=1, device_id=(me, following), device_id_type=MESH)
    pl.semaphore_signal(barrier, inc=1, device_id=(me, previous), device_id_type=MESH)

    @pl.when(seq == 0)
    def _():
        chain_recv[...] = jnp.zeros_like(chain_recv)

    pl.semaphore_wait(barrier, groups + 1)
    links = [
        pltpu.make_async_remote_copy(
            src_ref=chain_send.at[h], dst_ref=chain_recv.at[h], send_sem=chain_send_sem.at[h],
            recv_sem=chain_recv_sem.at[h], device_id=(me, following), device_id_type=MESH,
        )
        for h in range(heads)
    ]
    for h in range(heads):
        @pl.when(seq > 0)
        def _():
            links[h].wait_recv()

        @pl.when(seq < peers - 1)
        def _():
            before = chain_recv[h].astype(jnp.float32)
            chain_send[h] = (before * decay_ref[h : h + 1, :] + state_ref[h]).astype(jnp.bfloat16)
            links[h].start()

    def finished(target):
        slot = slot_for[target]
        for h in range(heads):
            cols = slice(h * size, (h + 1) * size)
            yield cols, (
                out_ref[slot, :, cols] + dot_nt(carry_ref[slot, :, cols], chain_recv[h])
            ).astype(jnp.bfloat16)

    copies = []
    for offset in ORDER:
        target = peer_along(offset, 1)
        for cols, part in finished(target):
            send[target, :, cols] = part
        copy = pltpu.make_async_remote_copy(
            src_ref=send.at[target], dst_ref=recv.at[me], send_sem=send_sem.at[target],
            recv_sem=recv_sem.at[me], device_id=(target, seq), device_id_type=MESH,
        )
        copy.start()
        copies.append(copy)
    for cols, part in finished(me):
        recv[me, :, cols] = part
    weight_copy.wait()
    sources = [me] + [peer_along(offset, -1) for offset in ORDER]
    together = gathered.shape[0] // piece_rows
    model_width = weight_held.shape[1]
    results = []
    for first in range(0, groups, together):
        for n in range(together):
            source = sources[first + n]
            if first + n > 0:
                pltpu.make_async_remote_copy(
                    src_ref=send.at[source], dst_ref=recv.at[source], send_sem=send_sem.at[source],
                    recv_sem=recv_sem.at[source], device_id=(source, seq), device_id_type=MESH,
                ).wait_recv()
            gathered[n * piece_rows : (n + 1) * piece_rows, :] = recv[source]
        tile = 512
        for start in range(0, model_width, tile):
            cols = slice(start, start + tile)
            product = jnp.dot(
                gathered[...], weight_held[:, cols], preferred_element_type=jnp.float32
            ).astype(jnp.bfloat16)
            for n in range(together):
                projected[sources[first + n], :, cols] = product[
                    n * piece_rows : (n + 1) * piece_rows
                ]
        for n in range(together):
            source = sources[first + n]
            copy = pltpu.make_async_copy(
                projected.at[source], result.at[source], result_sem.at[source]
            )
            copy.start()
            results.append(copy)
    for copy in results:
        copy.wait()
    for copy in copies:
        copy.wait_send()
    for h in range(heads):
        @pl.when(seq < peers - 1)
        def _():
            links[h].wait_send()


def give_back(slot_for, out, carry, state, decay, weight):
    groups = slot_for.shape[0]
    rows, width = out.shape
    piece_rows = rows // groups
    heads, size, _ = state.shape
    model_width = weight.shape[1]
    smem = pl.BlockSpec(memory_space=pltpu.SMEM)
    vmem = pl.BlockSpec(memory_space=pltpu.VMEM)
    hbm = pl.BlockSpec(memory_space=pl.ANY)
    pieces = (groups, piece_rows, width)
    return pl.pallas_call(
        return_kernel,
        out_shape=jax.ShapeDtypeStruct((groups, piece_rows, model_width), jnp.bfloat16),
        in_specs=[smem, vmem, vmem, vmem, vmem, hbm],
        out_specs=hbm,
        scratch_shapes=[
            pltpu.VMEM((heads, size, size), jnp.bfloat16),
            pltpu.VMEM((heads, size, size), jnp.bfloat16),
            pltpu.VMEM(pieces, jnp.bfloat16),
            pltpu.VMEM(pieces, jnp.bfloat16),
            pltpu.VMEM(weight.shape, jnp.bfloat16),
            pltpu.VMEM((4 * piece_rows, width), jnp.bfloat16),
            pltpu.VMEM((groups, piece_rows, model_width), jnp.bfloat16),
            pltpu.SemaphoreType.DMA,
            pltpu.SemaphoreType.DMA((heads,)),
            pltpu.SemaphoreType.DMA((heads,)),
            pltpu.SemaphoreType.DMA((groups,)),
            pltpu.SemaphoreType.DMA((groups,)),
            pltpu.SemaphoreType.DMA((groups,)),
        ],
        compiler_params=pltpu.CompilerParams(
            collective_id=1, has_side_effects=True, vmem_limit_bytes=50 << 20
        ),
    )(slot_for, out.reshape(pieces), carry.reshape(pieces), state, decay, weight)


def place_kernel(target_for, projected, result):
    result[...] = projected[...]


def place_pieces(target_for, projected):
    groups, piece_rows, model_width = projected.shape
    block = (1, piece_rows, model_width)
    return pl.pallas_call(
        place_kernel,
        out_shape=jax.ShapeDtypeStruct(projected.shape, projected.dtype),
        grid_spec=pltpu.PrefetchScalarGridSpec(
            num_scalar_prefetch=1,
            grid=(groups,),
            in_specs=[pl.BlockSpec(block, lambda n, target_for: (target_for[n], 0, 0))],
            out_specs=pl.BlockSpec(block, lambda n, target_for: (n, 0, 0)),
        ),
    )(target_for, projected)


def shards(
    tokens,
    norm_gain,
    qkv_weight,
    beta_weight,
    beta_bias,
    out_weight,
    doc_lengths,
    source_dp,
    source_offset,
):
    groups = lax.axis_size("dp")
    dp_index = lax.axis_index("dp")
    seq_index = lax.axis_index("seq")
    tok_dev, model_width = tokens.shape
    piece_rows = tok_dev // groups
    plan_source = lax.dynamic_index_in_dim(source_dp, seq_index, 1, keepdims=False)
    plan_offset = lax.dynamic_index_in_dim(source_offset, seq_index, 1, keepdims=False)
    from_here = plan_source == dp_index
    sent_piece = jnp.sum(jnp.where(from_here, plan_offset, 0), axis=1) // piece_rows
    slot_source = lax.dynamic_index_in_dim(plan_source, dp_index, 0, keepdims=False)
    query_rows, key_rows, value_rows, logits = arrive(
        sent_piece, tokens, norm_gain, qkv_weight, beta_weight, beta_bias
    )
    lengths = lax.dynamic_index_in_dim(doc_lengths, dp_index, 0, keepdims=False)
    starts = jnp.cumsum(lengths) - lengths
    place = (seq_index * tok_dev).astype(jnp.int32).reshape(1)
    heads_out, carried, local_state, decay_all = recurrence(
        slot_source, starts, place, query_rows, key_rows, value_rows, logits
    )
    numbers = jnp.arange(groups, dtype=jnp.int32)
    slot_for = jnp.sum(
        jnp.where(slot_source[None, :] == numbers[:, None], numbers[None, :], 0), axis=1
    )
    target_for = jnp.sum(
        jnp.where(sent_piece[None, :] == numbers[:, None], numbers[None, :], 0), axis=1
    )
    projected = give_back(slot_for, heads_out, carried, local_state, decay_all, out_weight)
    return place_pieces(target_for, projected).reshape(tok_dev, model_width)


def solution(mesh):
    return jax.shard_map(
        shards,
        mesh=mesh,
        in_specs=(P(("dp", "seq"), None), P(), P(), P(), P(), P(), P(), P(), P()),
        out_specs=P(("dp", "seq"), None),
        check_vma=False,
    )
```

```python
import jax
import jax.numpy as jnp
import numpy as np
from jax import lax
from jax.experimental import pallas as pl
from jax.experimental.pallas import tpu as pltpu
from jax.sharding import PartitionSpec as P

PIECE = 48
SUB = 12
TOGETHER = 4
MESH = pl.DeviceIdType.MESH
rms_epsilon = 1e-06
ORDER = [(1, 0), (3, 3), (2, 3), (1, 3), (1, 2), (0, 1), (2, 0), (3, 0), (3, 1), (2, 2), (0, 2), (3, 2), (1, 1), (0, 3), (2, 1)]


def decay_sums():
    row = np.arange(PIECE)[:, None]
    col = np.arange(PIECE)[None, :]

    def between(low, high):
        return ((col > low) & (col <= high)).astype(np.float32)

    mid = (row // SUB) * SUB + SUB // 2 - 1
    near = between(mid, row) - between(row, mid)
    half = (row // (2 * SUB)) * (2 * SUB) + SUB - 1
    pair = between(half, row) + between(row, half)
    middle = np.full_like(row, 2 * SUB - 1)
    whole = between(middle, row) + between(row, middle)
    before = between(np.full_like(row, -1), row)
    after = between(row, np.full_like(row, PIECE - 1))
    sums = np.concatenate([near, pair, whole, before, after], axis=0)
    return np.concatenate([sums, sums], axis=1)


def dot_nt(a, b):
    return lax.dot_general(a, b, (((1,), (1,)), ((), ())), preferred_element_type=jnp.float32)


def dot_tn(a, b):
    return lax.dot_general(a, b, (((0,), (0,)), ((), ())), preferred_element_type=jnp.float32)


def peer_along(offset, sign):
    me = lax.axis_index("dp")
    down, right = offset
    row = lax.rem(me // 4 + (down if sign > 0 else 4 - down), 4)
    column = lax.rem(lax.rem(me, 4) + (right if sign > 0 else 4 - right), 4)
    return row * 4 + column


def layer_kernel(
    sent, slot_of, rank_of, starts, tokens, gain_ref, weight, beta_ref, bias_ref, sums_ref,
    out_weight, result,
    held, send, recv, weight_held, out_weight_held, normed, qkv, strength_ref,
    out_ref, carry_ref, change_ref, decay_ref, state, total, prefix_ref, totals_ref,
    chain_send, chain_recv, back_send, back_recv, gathered,
    token_sem, weight_sem, out_weight_sem, send_sem, recv_sem,
    chain_send_sem, chain_recv_sem, back_send_sem, back_recv_sem, result_sem,
):
    groups, piece_rows, model_width = held.shape
    heads, size, _ = state.shape
    width = heads * size
    me, seq = lax.axis_index("dp"), lax.axis_index("seq")
    peers = lax.axis_size("seq")
    following, previous = lax.rem(seq + 1, peers), lax.rem(seq + peers - 1, peers)
    token_copy = pltpu.make_async_copy(tokens, held, token_sem)
    token_copy.start()
    weight_copy = pltpu.make_async_copy(weight, weight_held, weight_sem)
    out_weight_copy = pltpu.make_async_copy(out_weight, out_weight_held, out_weight_sem)
    barrier = pltpu.get_barrier_semaphore()
    for distance in range(1, groups):
        pl.semaphore_signal(
            barrier, inc=1, device_id=(lax.rem(me + distance, groups), seq), device_id_type=MESH
        )
    pl.semaphore_signal(barrier, inc=1, device_id=(me, following), device_id_type=MESH)
    pl.semaphore_signal(barrier, inc=1, device_id=(me, previous), device_id_type=MESH)
    token_copy.wait()
    weight_copy.start()
    out_weight_copy.start()
    send[0] = held[sent[me]]
    own_copy = pltpu.make_async_copy(send.at[0], recv.at[0], recv_sem.at[0])
    own_copy.start()

    @pl.when(seq == 0)
    def _():
        chain_recv[...] = jnp.zeros_like(chain_recv)

    pl.semaphore_wait(barrier, groups + 1)
    copies = []
    for n, offset in enumerate(ORDER):
        target = peer_along(offset, 1)
        send[n + 1] = held[sent[target]]
        copy = pltpu.make_async_remote_copy(
            src_ref=send.at[n + 1], dst_ref=recv.at[n + 1], send_sem=send_sem.at[n + 1],
            recv_sem=recv_sem.at[n + 1], device_id=(target, seq), device_id_type=MESH,
        )
        copy.start()
        copies.append(copy)
    weight_copy.wait()

    down = lax.broadcasted_iota(jnp.int32, (PIECE, PIECE), 0)
    across = lax.broadcasted_iota(jnp.int32, (PIECE, PIECE), 1)
    wide = lax.broadcasted_iota(jnp.int32, (PIECE, size), 0)
    causal = down >= across
    in_sub = causal & (down // SUB == across // SUB)
    in_pair = causal & (down // (2 * SUB) == across // (2 * SUB)) & (down // SUB != across // SUB)
    in_whole = causal & (down // (2 * SUB) != across // (2 * SUB))
    right_pair = (wide // SUB) % 2 == 1
    right_whole = wide >= 2 * SUB

    def document_of(position):
        count = jnp.zeros_like(position)
        for n in range(starts.shape[0]):
            count = count + (starts[n] <= position).astype(jnp.int32)
        return count

    def local_part(inside, rank):
        first = (seq * groups + slot_of[rank]) * PIECE
        doc_down = document_of(first + down)
        doc_across = document_of(first + across)
        doc_wide = document_of(first + wide)
        doc_before = document_of(first - 1)
        doc_last = document_of(first + PIECE - 1)
        same = doc_down == doc_across
        near_mask, pair_mask, whole_mask = in_sub & same, in_pair & same, in_whole & same
        reaches = (doc_wide == doc_before).astype(jnp.float32)
        stays = (doc_wide == doc_last).astype(jnp.float32)
        kept = (doc_last == doc_before).astype(jnp.float32)
        strength = strength_ref[inside]
        for h in range(heads):
            cols = slice(h * size, (h + 1) * size)
            query = qkv[0, inside, :, cols].astype(jnp.float32)
            key = qkv[1, inside, :, cols].astype(jnp.float32)
            value = qkv[2, inside, :, cols].astype(jnp.float32)
            squares = key * key
            now = strength[:, h : h + 1]
            step = now / (1.0 + now * jnp.sum(squares, axis=1, keepdims=True))
            log_decay = jnp.log(1.0 - step * squares)
            high = log_decay.astype(jnp.bfloat16)
            low = (log_decay - high.astype(jnp.float32)).astype(jnp.bfloat16)
            gaps = jnp.dot(
                sums_ref[...], jnp.concatenate([high, low], axis=0),
                preferred_element_type=jnp.float32,
            )
            near = gaps[:PIECE]
            pair = gaps[PIECE : 2 * PIECE]
            whole = gaps[2 * PIECE : 3 * PIECE]
            before = gaps[3 * PIECE : 4 * PIECE]
            after = gaps[4 * PIECE :]
            near_query = (query * jnp.exp(near)).astype(jnp.bfloat16)
            near_key = (key * jnp.exp(-near)).astype(jnp.bfloat16)
            pair_both = (jnp.where(right_pair, query, key) * jnp.exp(pair)).astype(jnp.bfloat16)
            whole_both = (jnp.where(right_whole, query, key) * jnp.exp(whole)).astype(jnp.bfloat16)
            scores = jnp.where(
                near_mask,
                dot_nt(near_query, near_key),
                jnp.where(
                    pair_mask,
                    dot_nt(pair_both, pair_both),
                    jnp.where(whole_mask, dot_nt(whole_both, whole_both), 0.0),
                ),
            )
            stepped = (value * step).astype(jnp.bfloat16)
            decayed = jnp.exp(before)
            out_ref[rank, :, cols] = jnp.dot(
                scores.astype(jnp.bfloat16), stepped, preferred_element_type=jnp.float32
            )
            carry_ref[rank, :, cols] = (query * (decayed * reaches)).astype(jnp.bfloat16)
            decay_ref[rank, h : h + 1, :] = decayed[PIECE - 1 :, :] * kept
            change_ref[rank, h] = dot_tn(
                stepped, (key * (jnp.exp(after) * stays)).astype(jnp.bfloat16)
            )

    @pl.loop(0, groups // TOGETHER)
    def _(group):
        for n in range(TOGETHER):
            rank = group * TOGETHER + n
            pltpu.make_async_copy(send.at[rank], recv.at[rank], recv_sem.at[rank]).wait()
            rows = recv[rank].astype(jnp.float32)
            normed[n * PIECE : (n + 1) * PIECE, :] = (
                rows
                * lax.rsqrt(jnp.mean(rows * rows, axis=1, keepdims=True) + rms_epsilon)
                * gain_ref[...]
            ).astype(jnp.bfloat16)
        logits = (
            jnp.dot(normed[...], beta_ref[...], preferred_element_type=jnp.float32) + bias_ref[...]
        )
        strength = 1.0 / (1.0 + jnp.exp(-logits))
        for n in range(TOGETHER):
            strength_ref[n] = strength[n * PIECE : (n + 1) * PIECE]
        tile = 512
        for part in range(3):
            for start in range(0, width, tile):
                cols = slice(start, start + tile)
                product = jnp.dot(
                    normed[...], weight_held[part, :, cols], preferred_element_type=jnp.float32
                ).astype(jnp.bfloat16)
                for n in range(TOGETHER):
                    qkv[part, n, :, cols] = product[n * PIECE : (n + 1) * PIECE]

        @pl.loop(0, TOGETHER)
        def _(inside):
            local_part(inside, group * TOGETHER + inside)

    state[...] = jnp.zeros_like(state)
    total[...] = jnp.ones_like(total)

    @pl.loop(0, groups)
    def _(slot):
        rank = rank_of[slot]
        for h in range(heads):
            prefix_ref[slot, h] = state[h].astype(jnp.bfloat16)
            state[h] = state[h] * decay_ref[rank, h : h + 1, :] + change_ref[rank, h]
        totals_ref[slot] = total[...]
        total[...] = total[...] * decay_ref[rank]

    def add_earlier(rank):
        slot = slot_of[rank]
        for h in range(heads):
            cols = slice(h * size, (h + 1) * size)
            carried = carry_ref[rank, :, cols]
            out_ref[rank, :, cols] += dot_nt(carried, prefix_ref[slot, h])
            carry_ref[rank, :, cols] = (
                carried.astype(jnp.float32) * totals_ref[slot, h : h + 1, :]
            ).astype(jnp.bfloat16)

    ahead = 2 * (seq + 1)
    pl.loop(0, ahead)(add_earlier)
    links = [
        pltpu.make_async_remote_copy(
            src_ref=chain_send.at[h], dst_ref=chain_recv.at[h], send_sem=chain_send_sem.at[h],
            recv_sem=chain_recv_sem.at[h], device_id=(me, following), device_id_type=MESH,
        )
        for h in range(heads)
    ]
    for h in range(heads):
        @pl.when(seq > 0)
        def _():
            links[h].wait_recv()

        @pl.when(seq < peers - 1)
        def _():
            before = chain_recv[h].astype(jnp.float32)
            chain_send[h] = (before * total[h : h + 1, :] + state[h]).astype(jnp.bfloat16)
            links[h].start()

    pl.loop(ahead, groups)(add_earlier)

    def finished(rank):
        for h in range(heads):
            cols = slice(h * size, (h + 1) * size)
            yield cols, (
                out_ref[rank, :, cols] + dot_nt(carry_ref[rank, :, cols], chain_recv[h])
            ).astype(jnp.bfloat16)

    for n, offset in enumerate(ORDER):
        for cols, part in finished(n + 1):
            back_send[n + 1, :, cols] = part
        copy = pltpu.make_async_remote_copy(
            src_ref=back_send.at[n + 1], dst_ref=back_recv.at[n + 1],
            send_sem=back_send_sem.at[n + 1], recv_sem=back_recv_sem.at[n + 1],
            device_id=(peer_along(offset, -1), seq), device_id_type=MESH,
        )
        copy.start()
        copies.append(copy)
    for cols, part in finished(0):
        back_send[0, :, cols] = part
    own_back = pltpu.make_async_copy(back_send.at[0], back_recv.at[0], back_recv_sem.at[0])
    own_back.start()
    out_weight_copy.wait()

    @pl.loop(0, groups // TOGETHER)
    def _(group):
        for n in range(TOGETHER):
            rank = group * TOGETHER + n
            pltpu.make_async_copy(
                back_send.at[rank], back_recv.at[rank], back_recv_sem.at[rank]
            ).wait()
            gathered[n * PIECE : (n + 1) * PIECE, :] = back_recv[rank]
        tile = 512
        for start in range(0, model_width, tile):
            cols = slice(start, start + tile)
            product = jnp.dot(
                gathered[...], out_weight_held[:, cols], preferred_element_type=jnp.float32
            ).astype(jnp.bfloat16)
            for n in range(TOGETHER):
                held[group * TOGETHER + n, :, cols] = product[n * PIECE : (n + 1) * PIECE]
        for n in range(TOGETHER):
            rank = group * TOGETHER + n
            pltpu.make_async_copy(held.at[rank], result.at[rank], result_sem.at[rank]).start()

    for rank in range(groups):
        pltpu.make_async_copy(held.at[rank], result.at[rank], result_sem.at[rank]).wait()
    for copy in copies:
        copy.wait_send()

    @pl.when(seq < peers - 1)
    def _():
        for link in links:
            link.wait_send()


def layer(sent, slot_of, rank_of, starts, tokens, gain, weight, beta, bias, out_weight):
    groups = sent.shape[0]
    rows, model_width = tokens.shape
    width = weight.shape[2]
    heads = beta.shape[1]
    size = width // heads
    smem = pl.BlockSpec(memory_space=pltpu.SMEM)
    vmem = pl.BlockSpec(memory_space=pltpu.VMEM)
    hbm = pl.BlockSpec(memory_space=pl.ANY)
    pieces = (groups, PIECE, model_width)
    narrow = (groups, PIECE, width)
    states = (heads, size, size)
    bfloat16, float32 = jnp.bfloat16, jnp.float32
    sems = pltpu.SemaphoreType.DMA((groups,))
    head_sems = pltpu.SemaphoreType.DMA((heads,))
    sums = jnp.asarray(decay_sums(), bfloat16)
    return pl.pallas_call(
        layer_kernel,
        out_shape=jax.ShapeDtypeStruct(pieces, bfloat16),
        in_specs=[smem] * 4 + [hbm, vmem, hbm, vmem, vmem, vmem, hbm],
        out_specs=hbm,
        scratch_shapes=[
            pltpu.VMEM(pieces, bfloat16),
            pltpu.VMEM(pieces, bfloat16),
            pltpu.VMEM(pieces, bfloat16),
            pltpu.VMEM(weight.shape, bfloat16),
            pltpu.VMEM(out_weight.shape, bfloat16),
            pltpu.VMEM((TOGETHER * PIECE, model_width), bfloat16),
            pltpu.VMEM((3, TOGETHER, PIECE, width), bfloat16),
            pltpu.VMEM((TOGETHER, PIECE, heads), float32),
            pltpu.VMEM(narrow, float32),
            pltpu.VMEM(narrow, bfloat16),
            pltpu.VMEM((groups,) + states, float32),
            pltpu.VMEM((groups, heads, size), float32),
            pltpu.VMEM(states, float32),
            pltpu.VMEM((heads, size), float32),
            pltpu.VMEM((groups,) + states, bfloat16),
            pltpu.VMEM((groups, heads, size), float32),
            pltpu.VMEM(states, bfloat16),
            pltpu.VMEM(states, bfloat16),
            pltpu.VMEM(narrow, bfloat16),
            pltpu.VMEM(narrow, bfloat16),
            pltpu.VMEM((TOGETHER * PIECE, width), bfloat16),
            pltpu.SemaphoreType.DMA,
            pltpu.SemaphoreType.DMA,
            pltpu.SemaphoreType.DMA,
            sems,
            sems,
            head_sems,
            head_sems,
            sems,
            sems,
            sems,
        ],
        compiler_params=pltpu.CompilerParams(
            collective_id=0, has_side_effects=True, vmem_limit_bytes=60 << 20
        ),
    )(
        sent, slot_of, rank_of, starts, tokens.reshape(pieces), gain.reshape(1, -1), weight, beta,
        bias.reshape(1, -1), sums, out_weight,
    )


def place_kernel(rank_for, projected, result, held, in_sems, out_sems):
    pieces = projected.shape[0]
    arrive = [
        pltpu.make_async_copy(projected.at[rank_for[n]], held.at[n], in_sems.at[n])
        for n in range(pieces)
    ]
    leave = [
        pltpu.make_async_copy(held.at[n], result.at[n], out_sems.at[n]) for n in range(pieces)
    ]
    for copy in arrive:
        copy.start()
    for n in range(pieces):
        arrive[n].wait()
        leave[n].start()
    for copy in leave:
        copy.wait()


def place_pieces(rank_for, projected):
    hbm = pl.BlockSpec(memory_space=pl.ANY)
    sems = pltpu.SemaphoreType.DMA((projected.shape[0],))
    return pl.pallas_call(
        place_kernel,
        out_shape=jax.ShapeDtypeStruct(projected.shape, projected.dtype),
        in_specs=[pl.BlockSpec(memory_space=pltpu.SMEM), hbm],
        out_specs=hbm,
        scratch_shapes=[pltpu.VMEM(projected.shape, projected.dtype), sems, sems],
    )(rank_for, projected)


def shards(
    tokens,
    norm_gain,
    qkv_weight,
    beta_weight,
    beta_bias,
    out_weight,
    doc_lengths,
    source_dp,
    source_offset,
):
    groups = lax.axis_size("dp")
    dp_index = lax.axis_index("dp")
    seq_index = lax.axis_index("seq")
    tok_dev, model_width = tokens.shape
    piece_rows = tok_dev // groups
    plan_source = lax.dynamic_index_in_dim(source_dp, seq_index, 1, keepdims=False)
    plan_offset = lax.dynamic_index_in_dim(source_offset, seq_index, 1, keepdims=False)
    from_here = plan_source == dp_index
    sent = jnp.sum(jnp.where(from_here, plan_offset, 0), axis=1) // piece_rows
    slot_source = lax.dynamic_index_in_dim(plan_source, dp_index, 0, keepdims=False)
    steps = np.asarray([(0, 0)] + ORDER, np.int32)

    def along(sign):
        return (dp_index // 4 + sign * steps[:, 0]) % 4 * 4 + (dp_index + sign * steps[:, 1]) % 4

    numbers = jnp.arange(groups, dtype=jnp.int32)
    from_rank = slot_source[:, None] == along(-1)[None, :]
    slot_of = jnp.sum(jnp.where(from_rank, numbers[:, None], 0), axis=0)
    rank_of = jnp.sum(jnp.where(from_rank, numbers[None, :], 0), axis=1)
    owned_piece = jnp.sum(
        jnp.where(along(1)[:, None] == numbers[None, :], sent[None, :], 0), axis=1
    )
    rank_for = jnp.sum(
        jnp.where(owned_piece[None, :] == numbers[:, None], numbers[None, :], 0), axis=1
    )
    lengths = lax.dynamic_index_in_dim(doc_lengths, dp_index, 0, keepdims=False)
    starts = jnp.cumsum(lengths) - lengths
    projected = layer(
        sent, slot_of, rank_of, starts, tokens, norm_gain, qkv_weight, beta_weight, beta_bias,
        out_weight,
    )
    return place_pieces(rank_for, projected).reshape(tok_dev, model_width)


def solution(mesh):
    return jax.shard_map(
        shards,
        mesh=mesh,
        in_specs=(P(("dp", "seq"), None), P(), P(), P(), P(), P(), P(), P(), P()),
        out_specs=P(("dp", "seq"), None),
        check_vma=False,
    )
```

```python
import jax
import jax.numpy as jnp
import numpy as np
from jax import lax
from jax.experimental import pallas as pl
from jax.experimental.pallas import tpu as pltpu
from jax.sharding import PartitionSpec as P

PIECE = 48
SUB = 12
TOGETHER = 4
WIDE = 12
LAST = 2
MESH = pl.DeviceIdType.MESH
rms_epsilon = 1e-06
ORDER = [(0, 1), (0, 3), (1, 0), (3, 0), (1, 1), (3, 3), (1, 3), (3, 1), (0, 2), (2, 0), (1, 2), (2, 3), (3, 2), (2, 1), (2, 2)]
WINDOW = 8
DOWN = sum(step[0] * 4**n for n, step in enumerate(ORDER))
RIGHT = sum(step[1] * 4**n for n, step in enumerate(ORDER))


def decay_sums():
    row = np.arange(PIECE)[:, None]
    col = np.arange(PIECE)[None, :]

    def between(low, high):
        return ((col > low) & (col <= high)).astype(np.float32)

    mid = (row // SUB) * SUB + SUB // 2 - 1
    near = between(mid, row) - between(row, mid)
    half = (row // (2 * SUB)) * (2 * SUB) + SUB - 1
    pair = between(half, row) + between(row, half)
    middle = np.full_like(row, 2 * SUB - 1)
    whole = between(middle, row) + between(row, middle)
    before = between(np.full_like(row, -1), row)[: 2 * SUB]
    after = between(row, np.full_like(row, PIECE - 1))[2 * SUB :]
    sums = np.concatenate([near, pair, whole, before, after], axis=0)
    return np.concatenate([sums, sums], axis=1)


def head_spread(heads, size):
    return np.tile(np.repeat(np.eye(heads, dtype=np.float32), size, axis=1), (3, 1))


def split(x):
    high = x.astype(jnp.bfloat16)
    return high, x - high.astype(jnp.float32)


def dot_nt(a, b):
    return lax.dot_general(a, b, (((1,), (1,)), ((), ())), preferred_element_type=jnp.float32)


def dot_tn(a, b):
    return lax.dot_general(a, b, (((0,), (0,)), ((), ())), preferred_element_type=jnp.float32)


def peer_along(rank, sign):
    me = lax.axis_index("dp")
    at = rank - 1
    power = 1 + 3 * (at % 2)
    power = power * (1 + 15 * (at // 2 % 2))
    power = power * (1 + 255 * (at // 4 % 2))
    power = power * (1 + 65535 * (at // 8))
    row = (me // 4 + 4 + sign * (DOWN // power % 4)) % 4
    column = (me % 4 + 4 + sign * (RIGHT // power % 4)) % 4
    return row * 4 + column


def peers_along(sign):
    me = lax.axis_index("dp")
    return [me] + [
        (me // 4 + 4 + sign * down) % 4 * 4 + (me % 4 + 4 + sign * right) % 4
        for down, right in ORDER
    ]


def layer_kernel(
    source_dp, source_offset, doc_lengths, tokens, gain_ref, weight, beta_ref, bias_ref, sums_ref,
    spread_ref, out_weight, result, rank_for,
    sent, slot_of, rank_of, starts, held, send, recv, weight_held, out_weight_held, normed, qkv, strength_ref, logs, gaps, stepped_ref, mixes,
    out_ref, carry_ref, change_ref, decay_ref, state, total, prefix_ref, totals_ref,
    chain_send, chain_recv, back_send, back_recv, gathered,
    token_sem, weight_sem, out_weight_sem, send_sem, recv_sem,
    chain_send_sem, chain_recv_sem, back_send_sem, back_recv_sem, result_sem,
):
    groups, piece_rows, model_width = held.shape
    heads, size, _ = state.shape
    width = heads * size
    me, seq = lax.axis_index("dp"), lax.axis_index("seq")
    peers = lax.axis_size("seq")
    following, previous = lax.rem(seq + 1, peers), lax.rem(seq + peers - 1, peers)

    def within(index):
        return jnp.clip(index, 0, groups - 1)

    token_copy = pltpu.make_async_copy(tokens, held, token_sem)
    token_copy.start()
    weight_copy = pltpu.make_async_copy(weight, weight_held, weight_sem)
    out_weight_copy = pltpu.make_async_copy(out_weight, out_weight_held, out_weight_sem)
    barrier = pltpu.get_barrier_semaphore()
    for distance in range(1, groups):
        pl.semaphore_signal(
            barrier, inc=1, device_id=(lax.rem(me + distance, groups), seq), device_id_type=MESH
        )
    pl.semaphore_signal(barrier, inc=1, device_id=(me, following), device_id_type=MESH)
    pl.semaphore_signal(barrier, inc=1, device_id=(me, previous), device_id_type=MESH)
    @pl.loop(0, groups)
    def _(target):
        offset = jnp.int32(0)
        for slot in range(groups):
            here = source_dp[target, seq, slot] == me
            offset = offset + jnp.where(here, source_offset[target, seq, slot], 0)
        sent[target] = offset // PIECE

    token_copy.wait()
    weight_copy.start()
    out_weight_copy.start()
    send[0] = held[within(sent[me])]
    own_copy = pltpu.make_async_copy(send.at[0], recv.at[0], recv_sem.at[0])
    own_copy.start()

    @pl.when(seq == 0)
    def _():
        chain_recv[...] = jnp.zeros_like(chain_recv)

    def arriving(rank):
        target = peer_along(rank, 1)
        return pltpu.make_async_remote_copy(
            src_ref=send.at[rank], dst_ref=recv.at[rank], send_sem=send_sem.at[rank],
            recv_sem=recv_sem.at[rank], device_id=(target, seq), device_id_type=MESH,
        )

    def launch(rank):
        send[rank] = held[within(sent[peer_along(rank, 1)])]
        arriving(rank).start()

    pl.semaphore_wait(barrier, groups + 1)
    pl.loop(1, WINDOW)(launch)
    sources = peers_along(-1)
    owners = peers_along(1)

    @pl.loop(0, groups)
    def _(slot):
        source = source_dp[me, seq, slot]
        rank = jnp.int32(0)
        for n in range(1, groups):
            rank = rank + jnp.where(source == sources[n], n, 0)
        rank_of[slot] = rank

    @pl.loop(0, groups)
    def _(rank):
        slot = jnp.int32(0)
        for n in range(1, groups):
            slot = slot + jnp.where(rank_of[n] == rank, n, 0)
        slot_of[rank] = slot

    @pl.loop(0, groups)
    def _(piece):
        rank = jnp.int32(0)
        for n in range(1, groups):
            rank = rank + jnp.where(sent[owners[n]] == piece, n, 0)
        rank_for[piece] = within(rank)

    begin = jnp.int32(0)
    for n in range(starts.shape[0]):
        starts[n] = begin
        begin = begin + doc_lengths[n, me]
    weight_copy.wait()

    down = lax.broadcasted_iota(jnp.int32, (PIECE, PIECE), 0)
    across = lax.broadcasted_iota(jnp.int32, (PIECE, PIECE), 1)
    wide = lax.broadcasted_iota(jnp.int32, (PIECE, size), 0)
    causal = down >= across
    in_sub = causal & (down // SUB == across // SUB)
    in_pair = causal & (down // (2 * SUB) == across // (2 * SUB)) & (down // SUB != across // SUB)
    in_whole = causal & (down // (2 * SUB) != across // (2 * SUB))
    right_pair = (wide // SUB) % 2 == 1

    def document_of(position):
        count = jnp.zeros_like(position)
        for n in range(starts.shape[0]):
            count = count + (starts[n] <= position).astype(jnp.int32)
        return count

    def local_part(inside, rank):
        first = (seq * groups + within(slot_of[rank])) * PIECE
        doc_down = document_of(first + down)
        doc_across = document_of(first + across)
        doc_wide = document_of(first + wide)
        doc_before = document_of(first - 1)
        doc_last = document_of(first + PIECE - 1)
        same = doc_down == doc_across
        near_mask, pair_mask, whole_mask = in_sub & same, in_pair & same, in_whole & same
        reaches = (doc_wide == doc_before).astype(jnp.float32)
        stays = (doc_wide == doc_last).astype(jnp.float32)
        kept = (doc_last == doc_before).astype(jnp.float32)
        head_cols = [slice(h * size, (h + 1) * size) for h in range(heads)]
        squares = []
        for cols in head_cols:
            key = qkv[1, inside, :, cols].astype(jnp.float32)
            high, low = split(key * key)
            squares.append(jnp.concatenate([high, low.astype(jnp.bfloat16)], axis=1))
        norms = jnp.dot(
            jnp.concatenate(squares, axis=0), jnp.ones((2 * size, size), jnp.bfloat16),
            preferred_element_type=jnp.float32,
        )
        for h, cols in enumerate(head_cols):
            key = qkv[1, inside, :, cols].astype(jnp.float32)
            now = strength_ref[inside, :, cols]
            step = now / (1.0 + now * norms[h * PIECE : (h + 1) * PIECE])
            stepped_ref[:, cols] = (qkv[2, inside, :, cols].astype(jnp.float32) * step).astype(
                jnp.bfloat16
            )
            high, low = split(jnp.log2(1.0 - step * (key * key)))
            logs[:PIECE, cols] = high
            logs[PIECE:, cols] = low.astype(jnp.bfloat16)
        for start in range(0, width, 2 * size):
            cols = slice(start, start + 2 * size)
            gaps[:, cols] = jnp.dot(
                sums_ref[...], logs[:, cols], preferred_element_type=jnp.float32
            )
        middle = 2 * SUB
        for h, cols in enumerate(head_cols):
            query = qkv[0, inside, :, cols].astype(jnp.float32)
            key = qkv[1, inside, :, cols].astype(jnp.float32)
            near = gaps[:PIECE, cols]
            mixes[0, :, cols] = (query * jnp.exp2(near)).astype(jnp.bfloat16)
            mixes[1, :, cols] = (key * jnp.exp2(-near)).astype(jnp.bfloat16)
            pair = jnp.exp2(gaps[PIECE : 2 * PIECE, cols])
            mixes[2, :, cols] = (jnp.where(right_pair, query, key) * pair).astype(jnp.bfloat16)
            whole = jnp.exp2(gaps[2 * PIECE : 3 * PIECE, cols])
            mixes[3, :, cols] = (
                jnp.concatenate([key[:middle], query[middle:]], axis=0) * whole
            ).astype(jnp.bfloat16)
            first_half = jnp.exp2(gaps[3 * PIECE : 3 * PIECE + middle, cols])
            second_half = jnp.exp2(gaps[3 * PIECE + middle :, cols])
            before = jnp.concatenate(
                [first_half, whole[middle:] * first_half[middle - 1 :]], axis=0
            )
            after = jnp.concatenate(
                [whole[:middle] * whole[PIECE - 1 :], second_half], axis=0
            )
            carry_ref[rank, :, cols] = (query * (before * reaches)).astype(jnp.bfloat16)
            mixes[4, :, cols] = (key * (after * stays)).astype(jnp.bfloat16)
            decay_ref[rank, h : h + 1, :] = before[PIECE - 1 :, :] * kept
        for h, cols in enumerate(head_cols):
            scores = jnp.where(
                near_mask,
                dot_nt(mixes[0, :, cols], mixes[1, :, cols]),
                jnp.where(
                    pair_mask,
                    dot_nt(mixes[2, :, cols], mixes[2, :, cols]),
                    jnp.where(whole_mask, dot_nt(mixes[3, :, cols], mixes[3, :, cols]), 0.0),
                ),
            )
            out_ref[rank, :, cols] = jnp.dot(
                scores.astype(jnp.bfloat16), stepped_ref[:, cols],
                preferred_element_type=jnp.float32,
            )
            change_ref[rank, h] = dot_tn(stepped_ref[:, cols], mixes[4, :, cols])

    def arrived(first, together):
        for n in range(together):
            rank = first + n
            pltpu.make_async_copy(send.at[rank], recv.at[rank], recv_sem.at[rank]).wait()

            @pl.when(rank + WINDOW < groups)
            def _():
                launch(rank + WINDOW)

            rows = recv[rank].astype(jnp.float32)
            normed[n * PIECE : (n + 1) * PIECE, :] = (
                rows
                * lax.rsqrt(jnp.mean(rows * rows, axis=1, keepdims=True) + rms_epsilon)
                * gain_ref[...]
            ).astype(jnp.bfloat16)
        rows_now = normed[: together * PIECE, :]
        strength = 1.0 / (1.0 + jnp.exp(-(dot_nt(rows_now, beta_ref[...]) + bias_ref[...])))
        high, rest = split(strength)
        middle, rest = split(rest)
        parts = jnp.concatenate([high, middle, rest.astype(jnp.bfloat16)], axis=1)
        for start in range(0, width, 2 * size):
            cols = slice(start, start + 2 * size)
            spread = jnp.dot(parts, spread_ref[:, cols], preferred_element_type=jnp.float32)
            for n in range(together):
                strength_ref[n, :, cols] = spread[n * PIECE : (n + 1) * PIECE]
        tile = 512
        for part in range(3):
            for start in range(0, width, tile):
                cols = slice(start, start + tile)
                product = jnp.dot(
                    rows_now, weight_held[part, :, cols], preferred_element_type=jnp.float32
                ).astype(jnp.bfloat16)
                for n in range(together):
                    qkv[part, n, :, cols] = product[n * PIECE : (n + 1) * PIECE]

        @pl.loop(0, together)
        def _(inside):
            local_part(inside, first + inside)

    @pl.loop(0, WIDE // TOGETHER)
    def _(group):
        arrived(group * TOGETHER, TOGETHER)

    @pl.loop(0, (groups - WIDE) // LAST)
    def _(group):
        arrived(WIDE + group * LAST, LAST)

    state[...] = jnp.zeros_like(state)
    total[...] = jnp.ones_like(total)

    @pl.loop(0, groups)
    def _(slot):
        rank = within(rank_of[slot])
        for h in range(heads):
            prefix_ref[slot, h] = state[h].astype(jnp.bfloat16)
            state[h] = state[h] * decay_ref[rank, h : h + 1, :] + change_ref[rank, h]
        totals_ref[slot] = total[...]
        total[...] = total[...] * decay_ref[rank]

    def add_earlier(rank):
        slot = within(slot_of[rank])
        for h in range(heads):
            cols = slice(h * size, (h + 1) * size)
            carried = carry_ref[rank, :, cols]
            out_ref[rank, :, cols] += dot_nt(carried, prefix_ref[slot, h])
            carry_ref[rank, :, cols] = (
                carried.astype(jnp.float32) * totals_ref[slot, h : h + 1, :]
            ).astype(jnp.bfloat16)

    ahead = 2 * (seq + 1)
    pl.loop(0, ahead)(add_earlier)
    links = [
        pltpu.make_async_remote_copy(
            src_ref=chain_send.at[h], dst_ref=chain_recv.at[h], send_sem=chain_send_sem.at[h],
            recv_sem=chain_recv_sem.at[h], device_id=(me, following), device_id_type=MESH,
        )
        for h in range(heads)
    ]
    for h in range(heads):
        @pl.when(seq > 0)
        def _():
            links[h].wait_recv()

        @pl.when(seq < peers - 1)
        def _():
            before = chain_recv[h].astype(jnp.float32)
            chain_send[h] = (before * total[h : h + 1, :] + state[h]).astype(jnp.bfloat16)
            links[h].start()

    pl.loop(ahead, groups)(add_earlier)

    def finished(rank):
        for h in range(heads):
            cols = slice(h * size, (h + 1) * size)
            yield cols, (
                out_ref[rank, :, cols] + dot_nt(carry_ref[rank, :, cols], chain_recv[h])
            ).astype(jnp.bfloat16)

    def leaving(rank):
        return pltpu.make_async_remote_copy(
            src_ref=back_send.at[rank], dst_ref=back_recv.at[rank],
            send_sem=back_send_sem.at[rank], recv_sem=back_recv_sem.at[rank],
            device_id=(peer_along(rank, -1), seq), device_id_type=MESH,
        )

    @pl.loop(1, groups)
    def _(rank):
        for cols, part in finished(rank):
            back_send[rank, :, cols] = part
        leaving(rank).start()

    for cols, part in finished(0):
        back_send[0, :, cols] = part
    own_back = pltpu.make_async_copy(back_send.at[0], back_recv.at[0], back_recv_sem.at[0])
    own_back.start()
    out_weight_copy.wait()

    @pl.loop(0, groups // TOGETHER)
    def _(group):
        for n in range(TOGETHER):
            rank = group * TOGETHER + n
            pltpu.make_async_copy(
                back_send.at[rank], back_recv.at[rank], back_recv_sem.at[rank]
            ).wait()
            gathered[n * PIECE : (n + 1) * PIECE, :] = back_recv[rank]
        tile = 512
        for start in range(0, model_width, tile):
            cols = slice(start, start + tile)
            product = jnp.dot(
                gathered[...], out_weight_held[:, cols], preferred_element_type=jnp.float32
            ).astype(jnp.bfloat16)
            for n in range(TOGETHER):
                held[group * TOGETHER + n, :, cols] = product[n * PIECE : (n + 1) * PIECE]
        for n in range(TOGETHER):
            rank = group * TOGETHER + n
            pltpu.make_async_copy(held.at[rank], result.at[rank], result_sem.at[rank]).start()

    for rank in range(groups):
        pltpu.make_async_copy(held.at[rank], result.at[rank], result_sem.at[rank]).wait()
    @pl.loop(1, groups)
    def _(rank):
        arriving(rank).wait_send()
        leaving(rank).wait_send()

    @pl.when(seq < peers - 1)
    def _():
        for link in links:
            link.wait_send()


def layer(
    source_dp, source_offset, doc_lengths, tokens, gain, weight, beta, bias, out_weight
):
    groups = source_dp.shape[0]
    rows, model_width = tokens.shape
    width = weight.shape[2]
    heads = beta.shape[1]
    size = width // heads
    smem = pl.BlockSpec(memory_space=pltpu.SMEM)
    vmem = pl.BlockSpec(memory_space=pltpu.VMEM)
    hbm = pl.BlockSpec(memory_space=pl.ANY)
    pieces = (groups, PIECE, model_width)
    narrow = (groups, PIECE, width)
    states = (heads, size, size)
    bfloat16, float32 = jnp.bfloat16, jnp.float32
    sems = pltpu.SemaphoreType.DMA((groups,))
    head_sems = pltpu.SemaphoreType.DMA((heads,))
    sums = jnp.asarray(decay_sums(), bfloat16)
    spread = jnp.asarray(head_spread(heads, size), bfloat16)
    return pl.pallas_call(
        layer_kernel,
        out_shape=(
            jax.ShapeDtypeStruct(pieces, bfloat16),
            jax.ShapeDtypeStruct((groups,), jnp.int32),
        ),
        in_specs=[smem] * 3 + [hbm, vmem, hbm, vmem, vmem, vmem, vmem, hbm],
        out_specs=(hbm, smem),
        scratch_shapes=[
            pltpu.SMEM((groups,), jnp.int32),
            pltpu.SMEM((groups,), jnp.int32),
            pltpu.SMEM((groups,), jnp.int32),
            pltpu.SMEM((doc_lengths.shape[0],), jnp.int32),
            pltpu.VMEM(pieces, bfloat16),
            pltpu.VMEM(pieces, bfloat16),
            pltpu.VMEM(pieces, bfloat16),
            pltpu.VMEM(weight.shape, bfloat16),
            pltpu.VMEM(out_weight.shape, bfloat16),
            pltpu.VMEM((TOGETHER * PIECE, model_width), bfloat16),
            pltpu.VMEM((3, TOGETHER, PIECE, width), bfloat16),
            pltpu.VMEM((TOGETHER, PIECE, width), float32),
            pltpu.VMEM((2 * PIECE, width), bfloat16),
            pltpu.VMEM((4 * PIECE, width), float32),
            pltpu.VMEM((PIECE, width), bfloat16),
            pltpu.VMEM((5, PIECE, width), bfloat16),
            pltpu.VMEM(narrow, float32),
            pltpu.VMEM(narrow, bfloat16),
            pltpu.VMEM((groups,) + states, float32),
            pltpu.VMEM((groups, heads, size), float32),
            pltpu.VMEM(states, float32),
            pltpu.VMEM((heads, size), float32),
            pltpu.VMEM((groups,) + states, bfloat16),
            pltpu.VMEM((groups, heads, size), float32),
            pltpu.VMEM(states, bfloat16),
            pltpu.VMEM(states, bfloat16),
            pltpu.VMEM(narrow, bfloat16),
            pltpu.VMEM(narrow, bfloat16),
            pltpu.VMEM((TOGETHER * PIECE, width), bfloat16),
            pltpu.SemaphoreType.DMA,
            pltpu.SemaphoreType.DMA,
            pltpu.SemaphoreType.DMA,
            sems,
            sems,
            head_sems,
            head_sems,
            sems,
            sems,
            sems,
        ],
        compiler_params=pltpu.CompilerParams(
            collective_id=0, has_side_effects=True, vmem_limit_bytes=60 << 20
        ),
    )(
        source_dp, source_offset, doc_lengths, tokens.reshape(pieces), gain.reshape(1, -1), weight,
        beta.T, bias.reshape(1, -1), sums, spread, out_weight,
    )


def place_kernel(rank_for, projected, result, held, in_sems, out_sems):
    pieces = projected.shape[0]
    arrive = [
        pltpu.make_async_copy(projected.at[jnp.clip(rank_for[n], 0, pieces - 1)], held.at[n], in_sems.at[n])
        for n in range(pieces)
    ]
    leave = [
        pltpu.make_async_copy(held.at[n], result.at[n], out_sems.at[n]) for n in range(pieces)
    ]
    for copy in arrive:
        copy.start()
    for n in range(pieces):
        arrive[n].wait()
        leave[n].start()
    for copy in leave:
        copy.wait()


def place_pieces(rank_for, projected):
    hbm = pl.BlockSpec(memory_space=pl.ANY)
    sems = pltpu.SemaphoreType.DMA((projected.shape[0],))
    return pl.pallas_call(
        place_kernel,
        out_shape=jax.ShapeDtypeStruct(projected.shape, projected.dtype),
        in_specs=[pl.BlockSpec(memory_space=pltpu.SMEM), hbm],
        out_specs=hbm,
        scratch_shapes=[pltpu.VMEM(projected.shape, projected.dtype), sems, sems],
    )(rank_for, projected)


def shards(
    tokens,
    norm_gain,
    qkv_weight,
    beta_weight,
    beta_bias,
    out_weight,
    doc_lengths,
    source_dp,
    source_offset,
):
    projected, rank_for = layer(
        source_dp, source_offset, doc_lengths.T, tokens, norm_gain, qkv_weight, beta_weight,
        beta_bias, out_weight,
    )
    return place_pieces(rank_for, projected).reshape(tokens.shape)


def solution(mesh):
    return jax.shard_map(
        shards,
        mesh=mesh,
        in_specs=(P(("dp", "seq"), None), P(), P(), P(), P(), P(), P(), P(), P()),
        out_specs=P(("dp", "seq"), None),
        check_vma=False,
    )
```

```python
import jax
import jax.numpy as jnp
import numpy as np
from jax import lax
from jax.experimental import pallas as pl
from jax.experimental.pallas import tpu as pltpu
from jax.sharding import PartitionSpec as P

PIECE = 48
SUB = 12
TOGETHER = 4
WIDE = 12
LAST = 2
MESH = pl.DeviceIdType.MESH
rms_epsilon = 1e-06
ORDER = [(0, 1), (0, 3), (1, 0), (3, 0), (1, 1), (3, 3), (1, 3), (3, 1), (0, 2), (2, 0), (1, 2), (2, 3), (3, 2), (2, 1), (2, 2)]
WINDOW = 8
DOWN = sum(step[0] * 4**n for n, step in enumerate(ORDER))
RIGHT = sum(step[1] * 4**n for n, step in enumerate(ORDER))


def decay_sums():
    row = np.arange(PIECE)[:, None]
    col = np.arange(PIECE)[None, :]

    def between(low, high):
        return ((col > low) & (col <= high)).astype(np.float32)

    mid = (row // SUB) * SUB + SUB // 2 - 1
    near = between(mid, row) - between(row, mid)
    half = (row // (2 * SUB)) * (2 * SUB) + SUB - 1
    pair = between(half, row) + between(row, half)
    middle = np.full_like(row, 2 * SUB - 1)
    whole = between(middle, row) + between(row, middle)
    before = between(np.full_like(row, -1), row)[: 2 * SUB]
    after = between(row, np.full_like(row, PIECE - 1))[2 * SUB :]
    sums = np.concatenate([near, pair, whole, before, after], axis=0)
    return np.concatenate([sums, sums], axis=1)


def split(x):
    high = x.astype(jnp.bfloat16)
    return high, x - high.astype(jnp.float32)


def dot_nt(a, b):
    return lax.dot_general(a, b, (((1,), (1,)), ((), ())), preferred_element_type=jnp.float32)


def dot_tn(a, b):
    return lax.dot_general(a, b, (((0,), (0,)), ((), ())), preferred_element_type=jnp.float32)


def peer_along(rank, sign):
    me = lax.axis_index("dp")
    at = rank - 1
    power = 1 + 3 * (at % 2)
    power = power * (1 + 15 * (at // 2 % 2))
    power = power * (1 + 255 * (at // 4 % 2))
    power = power * (1 + 65535 * (at // 8))
    row = (me // 4 + 4 + sign * (DOWN // power % 4)) % 4
    column = (me % 4 + 4 + sign * (RIGHT // power % 4)) % 4
    return row * 4 + column


def peers_along(sign):
    me = lax.axis_index("dp")
    return [me] + [
        (me // 4 + 4 + sign * down) % 4 * 4 + (me % 4 + 4 + sign * right) % 4
        for down, right in ORDER
    ]


def layer_kernel(
    source_dp, source_offset, doc_lengths, tokens, gain_ref, weight, beta_ref, bias_ref, sums_ref,
    out_weight, result, rank_for,
    sent, slot_of, rank_of, starts, held, send, recv, weight_held, out_weight_held, normed, qkv, strength_ref, logs, gaps, stepped_ref, mixes,
    out_ref, carry_ref, change_ref, decay_ref, state, total, prefix_ref, totals_ref,
    chain_send, chain_recv, chain_used, pair_recv, pair_total, back_send, back_recv, gathered,
    token_sem, weight_sem, out_weight_sem, send_sem, recv_sem,
    pair_sems, chip_sems, relay_sems, total_sems, back_send_sem, back_recv_sem, result_sem,
):
    groups, piece_rows, model_width = held.shape
    heads, size, _ = state.shape
    width = heads * size
    me, seq = lax.axis_index("dp"), lax.axis_index("seq")
    peers = lax.axis_size("seq")
    core, chip, chips = seq % 2, seq // 2, peers // 2
    partner = seq + 1 - 2 * core
    following, previous = (seq + 2) % peers, (seq + peers - 2) % peers

    def within(index):
        return jnp.clip(index, 0, groups - 1)

    token_copy = pltpu.make_async_copy(tokens, held, token_sem)
    token_copy.start()
    weight_copy = pltpu.make_async_copy(weight, weight_held, weight_sem)
    out_weight_copy = pltpu.make_async_copy(out_weight, out_weight_held, out_weight_sem)
    barrier = pltpu.get_barrier_semaphore()
    for distance in range(1, groups):
        pl.semaphore_signal(
            barrier, inc=1, device_id=(lax.rem(me + distance, groups), seq), device_id_type=MESH
        )
    pl.semaphore_signal(barrier, inc=1, device_id=(me, following), device_id_type=MESH)
    pl.semaphore_signal(barrier, inc=1, device_id=(me, previous), device_id_type=MESH)
    pl.semaphore_signal(barrier, inc=1, device_id=(me, partner), device_id_type=MESH)
    @pl.loop(0, groups)
    def _(target):
        offset = jnp.int32(0)
        for slot in range(groups):
            here = source_dp[target, seq, slot] == me
            offset = offset + jnp.where(here, source_offset[target, seq, slot], 0)
        sent[target] = offset // PIECE

    token_copy.wait()
    weight_copy.start()
    out_weight_copy.start()
    send[0] = held[within(sent[me])]
    own_copy = pltpu.make_async_copy(send.at[0], recv.at[0], recv_sem.at[0])
    own_copy.start()

    @pl.when(chip == 0)
    def _():
        chain_recv[...] = jnp.zeros_like(chain_recv)

    def arriving(rank):
        target = peer_along(rank, 1)
        return pltpu.make_async_remote_copy(
            src_ref=send.at[rank], dst_ref=recv.at[rank], send_sem=send_sem.at[rank],
            recv_sem=recv_sem.at[rank], device_id=(target, seq), device_id_type=MESH,
        )

    def launch(rank):
        send[rank] = held[within(sent[peer_along(rank, 1)])]
        arriving(rank).start()

    pl.semaphore_wait(barrier, groups + 2)
    pl.loop(1, WINDOW)(launch)
    sources = peers_along(-1)
    owners = peers_along(1)

    @pl.loop(0, groups)
    def _(slot):
        source = source_dp[me, seq, slot]
        rank = jnp.int32(0)
        for n in range(1, groups):
            rank = rank + jnp.where(source == sources[n], n, 0)
        rank_of[slot] = rank

    @pl.loop(0, groups)
    def _(rank):
        slot = jnp.int32(0)
        for n in range(1, groups):
            slot = slot + jnp.where(rank_of[n] == rank, n, 0)
        slot_of[rank] = slot

    @pl.loop(0, groups)
    def _(piece):
        rank = jnp.int32(0)
        for n in range(1, groups):
            rank = rank + jnp.where(sent[owners[n]] == piece, n, 0)
        rank_for[piece] = within(rank)

    begin = jnp.int32(0)
    for n in range(starts.shape[0]):
        starts[n] = begin
        begin = begin + doc_lengths[n, me]
    weight_copy.wait()

    down = lax.broadcasted_iota(jnp.int32, (PIECE, PIECE), 0)
    across = lax.broadcasted_iota(jnp.int32, (PIECE, PIECE), 1)
    wide = lax.broadcasted_iota(jnp.int32, (PIECE, size), 0)
    causal = down >= across
    in_sub = causal & (down // SUB == across // SUB)
    in_pair = causal & (down // (2 * SUB) == across // (2 * SUB)) & (down // SUB != across // SUB)
    in_whole = causal & (down // (2 * SUB) != across // (2 * SUB))
    right_pair = (wide // SUB) % 2 == 1

    def document_of(position):
        count = jnp.zeros_like(position)
        for n in range(starts.shape[0]):
            count = count + (starts[n] <= position).astype(jnp.int32)
        return count

    def local_part(inside, rank):
        first = (seq * groups + within(slot_of[rank])) * PIECE
        doc_down = document_of(first + down)
        doc_across = document_of(first + across)
        doc_wide = document_of(first + wide)
        doc_before = document_of(first - 1)
        doc_last = document_of(first + PIECE - 1)
        same = doc_down == doc_across
        near_mask, pair_mask, whole_mask = in_sub & same, in_pair & same, in_whole & same
        reaches = (doc_wide == doc_before).astype(jnp.float32)
        stays = (doc_wide == doc_last).astype(jnp.float32)
        kept = (doc_last == doc_before).astype(jnp.float32)
        head_cols = [slice(h * size, (h + 1) * size) for h in range(heads)]
        squares = []
        for cols in head_cols:
            key = qkv[1, inside, :, cols].astype(jnp.float32)
            high, low = split(key * key)
            squares.append(jnp.concatenate([high, low.astype(jnp.bfloat16)], axis=1))
        norms = jnp.dot(
            jnp.concatenate(squares, axis=0), jnp.ones((2 * size, size), jnp.bfloat16),
            preferred_element_type=jnp.float32,
        )
        for h, cols in enumerate(head_cols):
            key = qkv[1, inside, :, cols].astype(jnp.float32)
            now = strength_ref[inside, :, h : h + 1]
            step = now / (1.0 + now * norms[h * PIECE : (h + 1) * PIECE])
            stepped_ref[:, cols] = (qkv[2, inside, :, cols].astype(jnp.float32) * step).astype(
                jnp.bfloat16
            )
            high, low = split(jnp.log2(1.0 - step * (key * key)))
            logs[:PIECE, cols] = high
            logs[PIECE:, cols] = low.astype(jnp.bfloat16)
        for start in range(0, width, 2 * size):
            cols = slice(start, start + 2 * size)
            gaps[:, cols] = jnp.dot(
                sums_ref[...], logs[:, cols], preferred_element_type=jnp.float32
            )
        middle = 2 * SUB
        for h, cols in enumerate(head_cols):
            query = qkv[0, inside, :, cols].astype(jnp.float32)
            key = qkv[1, inside, :, cols].astype(jnp.float32)
            near = gaps[:PIECE, cols]
            mixes[0, :, cols] = (query * jnp.exp2(near)).astype(jnp.bfloat16)
            mixes[1, :, cols] = (key * jnp.exp2(-near)).astype(jnp.bfloat16)
            pair = jnp.exp2(gaps[PIECE : 2 * PIECE, cols])
            mixes[2, :, cols] = (jnp.where(right_pair, query, key) * pair).astype(jnp.bfloat16)
            whole = jnp.exp2(gaps[2 * PIECE : 3 * PIECE, cols])
            mixes[3, :, cols] = (
                jnp.concatenate([key[:middle], query[middle:]], axis=0) * whole
            ).astype(jnp.bfloat16)
            first_half = jnp.exp2(gaps[3 * PIECE : 3 * PIECE + middle, cols])
            second_half = jnp.exp2(gaps[3 * PIECE + middle :, cols])
            before = jnp.concatenate(
                [first_half, whole[middle:] * first_half[middle - 1 :]], axis=0
            )
            after = jnp.concatenate(
                [whole[:middle] * whole[PIECE - 1 :], second_half], axis=0
            )
            carry_ref[rank, :, cols] = (query * (before * reaches)).astype(jnp.bfloat16)
            mixes[4, :, cols] = (key * (after * stays)).astype(jnp.bfloat16)
            decay_ref[rank, h : h + 1, :] = before[PIECE - 1 :, :] * kept
        weights = []
        for cols in head_cols:
            scores = jnp.where(
                near_mask,
                dot_nt(mixes[0, :, cols], mixes[1, :, cols]),
                jnp.where(
                    pair_mask,
                    dot_nt(mixes[2, :, cols], mixes[2, :, cols]),
                    jnp.where(whole_mask, dot_nt(mixes[3, :, cols], mixes[3, :, cols]), 0.0),
                ),
            )
            weights.append(scores.astype(jnp.bfloat16))
        for h, cols in enumerate(head_cols):
            change_ref[rank, h] = dot_tn(stepped_ref[:, cols], mixes[4, :, cols])
        for h, cols in enumerate(head_cols):
            out_ref[rank, :, cols] = jnp.dot(
                weights[h], stepped_ref[:, cols], preferred_element_type=jnp.float32
            )

    def arrived(first, together):
        for n in range(together):
            rank = first + n
            pltpu.make_async_copy(send.at[rank], recv.at[rank], recv_sem.at[rank]).wait()

            @pl.when(rank + WINDOW < groups)
            def _():
                launch(rank + WINDOW)

            rows = recv[rank].astype(jnp.float32)
            normed[n * PIECE : (n + 1) * PIECE, :] = (
                rows
                * lax.rsqrt(jnp.mean(rows * rows, axis=1, keepdims=True) + rms_epsilon)
                * gain_ref[...]
            ).astype(jnp.bfloat16)
        rows_now = normed[: together * PIECE, :]
        strength = 1.0 / (1.0 + jnp.exp(-(dot_nt(rows_now, beta_ref[...]) + bias_ref[...])))
        for n in range(together):
            strength_ref[n] = strength[n * PIECE : (n + 1) * PIECE]
        tile = 512
        for part in range(3):
            for start in range(0, width, tile):
                cols = slice(start, start + tile)
                product = jnp.dot(
                    rows_now, weight_held[part, :, cols], preferred_element_type=jnp.float32
                ).astype(jnp.bfloat16)
                for n in range(together):
                    qkv[part, n, :, cols] = product[n * PIECE : (n + 1) * PIECE]

        @pl.loop(0, together)
        def _(inside):
            local_part(inside, first + inside)

    @pl.loop(0, WIDE // TOGETHER)
    def _(group):
        arrived(group * TOGETHER, TOGETHER)

    @pl.loop(0, (groups - WIDE) // LAST)
    def _(group):
        arrived(WIDE + group * LAST, LAST)

    state[...] = jnp.zeros_like(state)
    total[...] = jnp.ones_like(total)

    @pl.loop(0, groups)
    def _(slot):
        rank = within(rank_of[slot])
        for h in range(heads):
            prefix_ref[slot, h] = state[h].astype(jnp.bfloat16)
            state[h] = state[h] * decay_ref[rank, h : h + 1, :] + change_ref[rank, h]
        totals_ref[slot] = total[...]
        total[...] = total[...] * decay_ref[rank]

    def add_earlier(rank):
        slot = within(slot_of[rank])
        head_cols = [slice(h * size, (h + 1) * size) for h in range(heads)]
        carried = [carry_ref[rank, :, cols] for cols in head_cols]
        added = [
            out_ref[rank, :, cols] + dot_nt(carried[h], prefix_ref[slot, h])
            for h, cols in enumerate(head_cols)
        ]
        for h, cols in enumerate(head_cols):
            out_ref[rank, :, cols] = added[h]
            carry_ref[rank, :, cols] = (
                carried[h].astype(jnp.float32) * totals_ref[slot, h : h + 1, :]
            ).astype(jnp.bfloat16)

    def link(source, target, h, sems, peer):
        return pltpu.make_async_remote_copy(
            src_ref=source.at[h], dst_ref=target.at[h], send_sem=sems.at[0, h],
            recv_sem=sems.at[1, h], device_id=(me, peer), device_id_type=MESH,
        )

    def pair_link(h):
        return link(chain_send, pair_recv, h, pair_sems, partner)

    def chip_link(h):
        return link(chain_send, chain_recv, h, chip_sems, following)

    def relay_link(h):
        return link(chain_recv, chain_recv, h, relay_sems, partner)

    decay_link = pltpu.make_async_remote_copy(
        src_ref=total, dst_ref=pair_total, send_sem=total_sems.at[0], recv_sem=total_sems.at[1],
        device_id=(me, partner), device_id_type=MESH,
    )

    @pl.when(core == 0)
    def _():
        decay_link.start()
        for h in range(heads):
            chain_send[h] = state[h].astype(jnp.bfloat16)
            pair_link(h).start()

    pl.loop(0, groups)(add_earlier)

    @pl.when(core == 1)
    def _():
        decay_link.wait_recv()
        for h in range(heads):
            own_total = total[h : h + 1, :]
            both_total = own_total * pair_total[h : h + 1, :]
            pair_link(h).wait_recv()
            both_state = pair_recv[h].astype(jnp.float32) * own_total + state[h]

            @pl.when(chip > 0)
            def _():
                chip_link(h).wait_recv()

            @pl.when(chip < chips - 1)
            def _():
                before = chain_recv[h].astype(jnp.float32)
                chain_send[h] = (before * both_total + both_state).astype(jnp.bfloat16)
                chip_link(h).start()

            @pl.when(chip > 0)
            def _():
                relay_link(h).start()

        for h in range(heads):
            chain_used[h] = (
                chain_recv[h].astype(jnp.float32) * pair_total[h : h + 1, :]
                + pair_recv[h].astype(jnp.float32)
            ).astype(jnp.bfloat16)

    @pl.when(core == 0)
    def _():
        for h in range(heads):
            @pl.when(chip > 0)
            def _():
                relay_link(h).wait_recv()

            chain_used[h] = chain_recv[h]


    def finish(rank):
        head_cols = [slice(h * size, (h + 1) * size) for h in range(heads)]
        parts = [
            out_ref[rank, :, cols] + dot_nt(carry_ref[rank, :, cols], chain_used[h])
            for h, cols in enumerate(head_cols)
        ]
        for h, cols in enumerate(head_cols):
            back_send[rank, :, cols] = parts[h].astype(jnp.bfloat16)

    def leaving(rank):
        return pltpu.make_async_remote_copy(
            src_ref=back_send.at[rank], dst_ref=back_recv.at[rank],
            send_sem=back_send_sem.at[rank], recv_sem=back_recv_sem.at[rank],
            device_id=(peer_along(rank, -1), seq), device_id_type=MESH,
        )

    @pl.loop(1, groups)
    def _(rank):
        finish(rank)
        leaving(rank).start()

    finish(0)
    own_back = pltpu.make_async_copy(back_send.at[0], back_recv.at[0], back_recv_sem.at[0])
    own_back.start()
    out_weight_copy.wait()

    @pl.loop(0, groups // TOGETHER)
    def _(group):
        for n in range(TOGETHER):
            rank = group * TOGETHER + n
            pltpu.make_async_copy(
                back_send.at[rank], back_recv.at[rank], back_recv_sem.at[rank]
            ).wait()
            gathered[n * PIECE : (n + 1) * PIECE, :] = back_recv[rank]
        tile = 512
        for start in range(0, model_width, tile):
            cols = slice(start, start + tile)
            product = jnp.dot(
                gathered[...], out_weight_held[:, cols], preferred_element_type=jnp.float32
            ).astype(jnp.bfloat16)
            for n in range(TOGETHER):
                held[group * TOGETHER + n, :, cols] = product[n * PIECE : (n + 1) * PIECE]
        for n in range(TOGETHER):
            rank = group * TOGETHER + n
            pltpu.make_async_copy(held.at[rank], result.at[rank], result_sem.at[rank]).start()

    for rank in range(groups):
        pltpu.make_async_copy(held.at[rank], result.at[rank], result_sem.at[rank]).wait()
    @pl.loop(1, groups)
    def _(rank):
        arriving(rank).wait_send()
        leaving(rank).wait_send()

    @pl.when(core == 0)
    def _():
        decay_link.wait_send()
        for h in range(heads):
            pair_link(h).wait_send()

    @pl.when(core == 1)
    def _():
        for h in range(heads):
            @pl.when(chip < chips - 1)
            def _():
                chip_link(h).wait_send()

            @pl.when(chip > 0)
            def _():
                relay_link(h).wait_send()


def layer(
    source_dp, source_offset, doc_lengths, tokens, gain, weight, beta, bias, out_weight
):
    groups = source_dp.shape[0]
    rows, model_width = tokens.shape
    width = weight.shape[2]
    heads = beta.shape[1]
    size = width // heads
    smem = pl.BlockSpec(memory_space=pltpu.SMEM)
    vmem = pl.BlockSpec(memory_space=pltpu.VMEM)
    hbm = pl.BlockSpec(memory_space=pl.ANY)
    pieces = (groups, PIECE, model_width)
    narrow = (groups, PIECE, width)
    states = (heads, size, size)
    bfloat16, float32 = jnp.bfloat16, jnp.float32
    sems = pltpu.SemaphoreType.DMA((groups,))
    head_sems = pltpu.SemaphoreType.DMA((2, heads))
    sums = jnp.asarray(decay_sums(), bfloat16)
    return pl.pallas_call(
        layer_kernel,
        out_shape=(
            jax.ShapeDtypeStruct(pieces, bfloat16),
            jax.ShapeDtypeStruct((groups,), jnp.int32),
        ),
        in_specs=[smem] * 3 + [hbm, vmem, hbm, vmem, vmem, vmem, hbm],
        out_specs=(hbm, smem),
        scratch_shapes=[
            pltpu.SMEM((groups,), jnp.int32),
            pltpu.SMEM((groups,), jnp.int32),
            pltpu.SMEM((groups,), jnp.int32),
            pltpu.SMEM((doc_lengths.shape[0],), jnp.int32),
            pltpu.VMEM(pieces, bfloat16),
            pltpu.VMEM(pieces, bfloat16),
            pltpu.VMEM(pieces, bfloat16),
            pltpu.VMEM(weight.shape, bfloat16),
            pltpu.VMEM(out_weight.shape, bfloat16),
            pltpu.VMEM((TOGETHER * PIECE, model_width), bfloat16),
            pltpu.VMEM((3, TOGETHER, PIECE, width), bfloat16),
            pltpu.VMEM((TOGETHER, PIECE, heads), float32),
            pltpu.VMEM((2 * PIECE, width), bfloat16),
            pltpu.VMEM((4 * PIECE, width), float32),
            pltpu.VMEM((PIECE, width), bfloat16),
            pltpu.VMEM((5, PIECE, width), bfloat16),
            pltpu.VMEM(narrow, float32),
            pltpu.VMEM(narrow, bfloat16),
            pltpu.VMEM((groups,) + states, float32),
            pltpu.VMEM((groups, heads, size), float32),
            pltpu.VMEM(states, float32),
            pltpu.VMEM((heads, size), float32),
            pltpu.VMEM((groups,) + states, bfloat16),
            pltpu.VMEM((groups, heads, size), float32),
            pltpu.VMEM(states, bfloat16),
            pltpu.VMEM(states, bfloat16),
            pltpu.VMEM(states, bfloat16),
            pltpu.VMEM(states, bfloat16),
            pltpu.VMEM((heads, size), float32),
            pltpu.VMEM(narrow, bfloat16),
            pltpu.VMEM(narrow, bfloat16),
            pltpu.VMEM((TOGETHER * PIECE, width), bfloat16),
            pltpu.SemaphoreType.DMA,
            pltpu.SemaphoreType.DMA,
            pltpu.SemaphoreType.DMA,
            sems,
            sems,
            head_sems,
            head_sems,
            head_sems,
            pltpu.SemaphoreType.DMA((2,)),
            sems,
            sems,
            sems,
        ],
        compiler_params=pltpu.CompilerParams(
            collective_id=0, has_side_effects=True, vmem_limit_bytes=60 << 20
        ),
    )(
        source_dp, source_offset, doc_lengths, tokens.reshape(pieces), gain.reshape(1, -1), weight,
        beta.T, bias.reshape(1, -1), sums, out_weight,
    )


def place_kernel(rank_for, projected, result, held, in_sems, out_sems):
    pieces = projected.shape[0]
    arrive = [
        pltpu.make_async_copy(projected.at[jnp.clip(rank_for[n], 0, pieces - 1)], held.at[n], in_sems.at[n])
        for n in range(pieces)
    ]
    leave = [
        pltpu.make_async_copy(held.at[n], result.at[n], out_sems.at[n]) for n in range(pieces)
    ]
    for copy in arrive:
        copy.start()
    for n in range(pieces):
        arrive[n].wait()
        leave[n].start()
    for copy in leave:
        copy.wait()


def place_pieces(rank_for, projected):
    hbm = pl.BlockSpec(memory_space=pl.ANY)
    sems = pltpu.SemaphoreType.DMA((projected.shape[0],))
    return pl.pallas_call(
        place_kernel,
        out_shape=jax.ShapeDtypeStruct(projected.shape, projected.dtype),
        in_specs=[pl.BlockSpec(memory_space=pltpu.SMEM), hbm],
        out_specs=hbm,
        scratch_shapes=[pltpu.VMEM(projected.shape, projected.dtype), sems, sems],
    )(rank_for, projected)


def shards(
    tokens,
    norm_gain,
    qkv_weight,
    beta_weight,
    beta_bias,
    out_weight,
    doc_lengths,
    source_dp,
    source_offset,
):
    projected, rank_for = layer(
        source_dp, source_offset, doc_lengths.T, tokens, norm_gain, qkv_weight, beta_weight,
        beta_bias, out_weight,
    )
    return place_pieces(rank_for, projected).reshape(tokens.shape)


def solution(mesh):
    return jax.shard_map(
        shards,
        mesh=mesh,
        in_specs=(P(("dp", "seq"), None), P(), P(), P(), P(), P(), P(), P(), P()),
        out_specs=P(("dp", "seq"), None),
        check_vma=False,
    )
```

```python
import jax
import jax.numpy as jnp
import numpy as np
from jax import lax
from jax.experimental import pallas as pl
from jax.experimental.pallas import tpu as pltpu
from jax.sharding import PartitionSpec as P

PIECE = 48
SUB = 12
TOGETHER = 4
WIDE = 12
LAST = 2
MESH = pl.DeviceIdType.MESH
rms_epsilon = 1e-06
ORDER = [(0, 1), (0, 3), (1, 0), (3, 0), (1, 1), (3, 3), (1, 3), (3, 1), (0, 2), (2, 0), (1, 2), (2, 3), (3, 2), (2, 1), (2, 2)]
WINDOW = 8
DOWN = sum(step[0] * 4**n for n, step in enumerate(ORDER))
RIGHT = sum(step[1] * 4**n for n, step in enumerate(ORDER))


def decay_sums():
    row = np.arange(PIECE)[:, None]
    col = np.arange(PIECE)[None, :]

    def between(low, high):
        return ((col > low) & (col <= high)).astype(np.float32)

    mid = (row // SUB) * SUB + SUB // 2 - 1
    near = between(mid, row) - between(row, mid)
    half = (row // (2 * SUB)) * (2 * SUB) + SUB - 1
    pair = between(half, row) + between(row, half)
    middle = np.full_like(row, 2 * SUB - 1)
    whole = between(middle, row) + between(row, middle)
    before = between(np.full_like(row, -1), row)[: 2 * SUB]
    after = between(row, np.full_like(row, PIECE - 1))[2 * SUB :]
    sums = np.concatenate([near, pair, whole, before, after], axis=0)
    return np.concatenate([sums, sums], axis=1)


def split(x):
    high = x.astype(jnp.bfloat16)
    return high, x - high.astype(jnp.float32)


def dot_nt(a, b):
    return lax.dot_general(a, b, (((1,), (1,)), ((), ())), preferred_element_type=jnp.float32)


def dot_tn(a, b):
    return lax.dot_general(a, b, (((0,), (0,)), ((), ())), preferred_element_type=jnp.float32)


def peer_along(rank, sign):
    me = lax.axis_index("dp")
    at = rank - 1
    power = 1 + 3 * (at % 2)
    power = power * (1 + 15 * (at // 2 % 2))
    power = power * (1 + 255 * (at // 4 % 2))
    power = power * (1 + 65535 * (at // 8))
    row = (me // 4 + 4 + sign * (DOWN // power % 4)) % 4
    column = (me % 4 + 4 + sign * (RIGHT // power % 4)) % 4
    return row * 4 + column


def peers_along(sign):
    me = lax.axis_index("dp")
    return [me] + [
        (me // 4 + 4 + sign * down) % 4 * 4 + (me % 4 + 4 + sign * right) % 4
        for down, right in ORDER
    ]


def layer_kernel(
    source_dp, source_offset, doc_lengths, tokens, gain_ref, weight, beta_ref, bias_ref, sums_ref,
    out_weight, result, rank_for,
    sent, slot_of, rank_of, starts, held, send, recv, weight_held, out_weight_held, normed, qkv, strength_ref, logs, gaps, stepped_ref, mixes,
    out_ref, carry_ref, change_ref, decay_ref, state, total, prefix_ref, totals_ref,
    chain_send, chain_recv, chain_used, pair_recv, pair_total, back_send, back_recv, gathered,
    token_sem, weight_sem, out_weight_sem, send_sem, recv_sem,
    pair_sems, chip_sems, relay_sems, total_sems, back_send_sem, back_recv_sem, result_sem,
):
    groups, piece_rows, model_width = held.shape
    heads, size, _ = state.shape
    width = heads * size
    me, seq = lax.axis_index("dp"), lax.axis_index("seq")
    peers = lax.axis_size("seq")
    core, chip, chips = seq % 2, seq // 2, peers // 2
    partner = seq + 1 - 2 * core
    following, previous = (seq + 2) % peers, (seq + peers - 2) % peers

    def within(index):
        return jnp.clip(index, 0, groups - 1)

    token_copy = pltpu.make_async_copy(tokens, held, token_sem)
    token_copy.start()
    weight_copy = pltpu.make_async_copy(weight, weight_held, weight_sem)
    out_weight_copy = pltpu.make_async_copy(out_weight, out_weight_held, out_weight_sem)
    barrier = pltpu.get_barrier_semaphore()
    for distance in range(1, groups):
        pl.semaphore_signal(
            barrier, inc=1, device_id=(lax.rem(me + distance, groups), seq), device_id_type=MESH
        )
    pl.semaphore_signal(barrier, inc=1, device_id=(me, following), device_id_type=MESH)
    pl.semaphore_signal(barrier, inc=1, device_id=(me, previous), device_id_type=MESH)
    pl.semaphore_signal(barrier, inc=1, device_id=(me, partner), device_id_type=MESH)
    @pl.loop(0, groups)
    def _(target):
        offset = jnp.int32(0)
        for slot in range(groups):
            here = source_dp[target, seq, slot] == me
            offset = offset + jnp.where(here, source_offset[target, seq, slot], 0)
        sent[target] = offset // PIECE

    token_copy.wait()
    weight_copy.start()
    out_weight_copy.start()
    send[0] = held[within(sent[me])]
    own_copy = pltpu.make_async_copy(send.at[0], recv.at[0], recv_sem.at[0])
    own_copy.start()

    @pl.when(chip == 0)
    def _():
        chain_recv[...] = jnp.zeros_like(chain_recv)

    def arriving(rank):
        target = peer_along(rank, 1)
        return pltpu.make_async_remote_copy(
            src_ref=send.at[rank], dst_ref=recv.at[rank], send_sem=send_sem.at[rank],
            recv_sem=recv_sem.at[rank], device_id=(target, seq), device_id_type=MESH,
        )

    def stage(rank):
        send[rank] = held[within(sent[peer_along(rank, 1)])]

    def launch(rank):
        stage(rank)
        arriving(rank).start()

    pl.loop(1, WINDOW)(stage)
    pl.semaphore_wait(barrier, groups + 2)

    @pl.loop(1, WINDOW)
    def _(rank):
        arriving(rank).start()

    sources = peers_along(-1)
    owners = peers_along(1)

    @pl.loop(0, groups)
    def _(slot):
        source = source_dp[me, seq, slot]
        rank = jnp.int32(0)
        for n in range(1, groups):
            rank = rank + jnp.where(source == sources[n], n, 0)
        rank_of[slot] = rank

    @pl.loop(0, groups)
    def _(rank):
        slot = jnp.int32(0)
        for n in range(1, groups):
            slot = slot + jnp.where(rank_of[n] == rank, n, 0)
        slot_of[rank] = slot

    @pl.loop(0, groups)
    def _(piece):
        rank = jnp.int32(0)
        for n in range(1, groups):
            rank = rank + jnp.where(sent[owners[n]] == piece, n, 0)
        rank_for[piece] = within(rank)

    begin = jnp.int32(0)
    for n in range(starts.shape[0]):
        starts[n] = begin
        begin = begin + doc_lengths[n, me]
    weight_copy.wait()

    down = lax.broadcasted_iota(jnp.int32, (PIECE, PIECE), 0)
    across = lax.broadcasted_iota(jnp.int32, (PIECE, PIECE), 1)
    wide = lax.broadcasted_iota(jnp.int32, (PIECE, size), 0)
    causal = down >= across
    in_sub = causal & (down // SUB == across // SUB)
    in_pair = causal & (down // (2 * SUB) == across // (2 * SUB)) & (down // SUB != across // SUB)
    in_whole = causal & (down // (2 * SUB) != across // (2 * SUB))
    right_pair = (wide // SUB) % 2 == 1

    def document_of(position):
        count = jnp.zeros_like(position)
        for n in range(starts.shape[0]):
            count = count + (starts[n] <= position).astype(jnp.int32)
        return count

    def local_part(inside, rank):
        first = (seq * groups + within(slot_of[rank])) * PIECE
        doc_down = document_of(first + down)
        doc_across = document_of(first + across)
        doc_wide = document_of(first + wide)
        doc_before = document_of(first - 1)
        doc_last = document_of(first + PIECE - 1)
        same = doc_down == doc_across
        near_mask, pair_mask, whole_mask = in_sub & same, in_pair & same, in_whole & same
        reaches = (doc_wide == doc_before).astype(jnp.float32)
        stays = (doc_wide == doc_last).astype(jnp.float32)
        kept = (doc_last == doc_before).astype(jnp.float32)
        head_cols = [slice(h * size, (h + 1) * size) for h in range(heads)]
        squares = []
        for cols in head_cols:
            key = qkv[1, inside, :, cols].astype(jnp.float32)
            high, low = split(key * key)
            squares.append(jnp.concatenate([high, low.astype(jnp.bfloat16)], axis=1))
        norms = jnp.dot(
            jnp.concatenate(squares, axis=0), jnp.ones((2 * size, size), jnp.bfloat16),
            preferred_element_type=jnp.float32,
        )
        for h, cols in enumerate(head_cols):
            key = qkv[1, inside, :, cols].astype(jnp.float32)
            now = strength_ref[inside, :, h : h + 1]
            step = now / (1.0 + now * norms[h * PIECE : (h + 1) * PIECE])
            stepped_ref[:, cols] = (qkv[2, inside, :, cols].astype(jnp.float32) * step).astype(
                jnp.bfloat16
            )
            high, low = split(jnp.log2(1.0 - step * (key * key)))
            logs[:PIECE, cols] = high
            logs[PIECE:, cols] = low.astype(jnp.bfloat16)
        for start in range(0, width, 2 * size):
            cols = slice(start, start + 2 * size)
            gaps[:, cols] = jnp.dot(
                sums_ref[...], logs[:, cols], preferred_element_type=jnp.float32
            )
        middle = 2 * SUB
        for h, cols in enumerate(head_cols):
            query = qkv[0, inside, :, cols].astype(jnp.float32)
            key = qkv[1, inside, :, cols].astype(jnp.float32)
            near = gaps[:PIECE, cols]
            mixes[0, :, cols] = (query * jnp.exp2(near)).astype(jnp.bfloat16)
            mixes[1, :, cols] = (key * jnp.exp2(-near)).astype(jnp.bfloat16)
            pair = jnp.exp2(gaps[PIECE : 2 * PIECE, cols])
            mixes[2, :, cols] = (jnp.where(right_pair, query, key) * pair).astype(jnp.bfloat16)
            whole = jnp.exp2(gaps[2 * PIECE : 3 * PIECE, cols])
            mixes[3, :, cols] = (
                jnp.concatenate([key[:middle], query[middle:]], axis=0) * whole
            ).astype(jnp.bfloat16)
            first_half = jnp.exp2(gaps[3 * PIECE : 3 * PIECE + middle, cols])
            second_half = jnp.exp2(gaps[3 * PIECE + middle :, cols])
            before = jnp.concatenate(
                [first_half, whole[middle:] * first_half[middle - 1 :]], axis=0
            )
            after = jnp.concatenate(
                [whole[:middle] * whole[PIECE - 1 :], second_half], axis=0
            )
            carry_ref[rank, :, cols] = (query * (before * reaches)).astype(jnp.bfloat16)
            mixes[4, :, cols] = (key * (after * stays)).astype(jnp.bfloat16)
            decay_ref[rank, h : h + 1, :] = before[PIECE - 1 :, :] * kept
        weights = []
        for cols in head_cols:
            scores = jnp.where(
                near_mask,
                dot_nt(mixes[0, :, cols], mixes[1, :, cols]),
                jnp.where(
                    pair_mask,
                    dot_nt(mixes[2, :, cols], mixes[2, :, cols]),
                    jnp.where(whole_mask, dot_nt(mixes[3, :, cols], mixes[3, :, cols]), 0.0),
                ),
            )
            weights.append(scores.astype(jnp.bfloat16))
        for h, cols in enumerate(head_cols):
            change_ref[rank, h] = dot_tn(stepped_ref[:, cols], mixes[4, :, cols])
        for h, cols in enumerate(head_cols):
            out_ref[rank, :, cols] = jnp.dot(
                weights[h], stepped_ref[:, cols], preferred_element_type=jnp.float32
            )

    def arrived(first, together):
        for n in range(together):
            rank = first + n
            pltpu.make_async_copy(send.at[rank], recv.at[rank], recv_sem.at[rank]).wait()

            @pl.when(rank + WINDOW < groups)
            def _():
                launch(rank + WINDOW)

            rows = recv[rank].astype(jnp.float32)
            normed[n * PIECE : (n + 1) * PIECE, :] = (
                rows
                * lax.rsqrt(jnp.mean(rows * rows, axis=1, keepdims=True) + rms_epsilon)
                * gain_ref[...]
            ).astype(jnp.bfloat16)
        rows_now = normed[: together * PIECE, :]
        strength = 1.0 / (1.0 + jnp.exp(-(dot_nt(rows_now, beta_ref[...]) + bias_ref[...])))
        for n in range(together):
            strength_ref[n] = strength[n * PIECE : (n + 1) * PIECE]
        tile = 512
        for part in range(3):
            for start in range(0, width, tile):
                cols = slice(start, start + tile)
                product = jnp.dot(
                    rows_now, weight_held[part, :, cols], preferred_element_type=jnp.float32
                ).astype(jnp.bfloat16)
                for n in range(together):
                    qkv[part, n, :, cols] = product[n * PIECE : (n + 1) * PIECE]

        @pl.loop(0, together)
        def _(inside):
            local_part(inside, first + inside)

    @pl.loop(0, WIDE // TOGETHER)
    def _(group):
        arrived(group * TOGETHER, TOGETHER)

    @pl.loop(0, (groups - WIDE) // LAST)
    def _(group):
        arrived(WIDE + group * LAST, LAST)

    state[...] = jnp.zeros_like(state)
    total[...] = jnp.ones_like(total)

    @pl.loop(0, groups)
    def _(slot):
        rank = within(rank_of[slot])
        for h in range(heads):
            prefix_ref[slot, h] = state[h].astype(jnp.bfloat16)
            state[h] = state[h] * decay_ref[rank, h : h + 1, :] + change_ref[rank, h]
        totals_ref[slot] = total[...]
        total[...] = total[...] * decay_ref[rank]

    def add_earlier(rank):
        slot = within(slot_of[rank])
        head_cols = [slice(h * size, (h + 1) * size) for h in range(heads)]
        carried = [carry_ref[rank, :, cols] for cols in head_cols]
        added = [
            out_ref[rank, :, cols] + dot_nt(carried[h], prefix_ref[slot, h])
            for h, cols in enumerate(head_cols)
        ]
        for h, cols in enumerate(head_cols):
            out_ref[rank, :, cols] = added[h]
            carry_ref[rank, :, cols] = (
                carried[h].astype(jnp.float32) * totals_ref[slot, h : h + 1, :]
            ).astype(jnp.bfloat16)

    def link(source, target, h, sems, peer):
        return pltpu.make_async_remote_copy(
            src_ref=source.at[h], dst_ref=target.at[h], send_sem=sems.at[0, h],
            recv_sem=sems.at[1, h], device_id=(me, peer), device_id_type=MESH,
        )

    def pair_link(h):
        return link(chain_send, pair_recv, h, pair_sems, partner)

    def chip_link(h):
        return link(chain_send, chain_recv, h, chip_sems, following)

    def relay_link(h):
        return link(chain_recv, chain_recv, h, relay_sems, partner)

    decay_link = pltpu.make_async_remote_copy(
        src_ref=total, dst_ref=pair_total, send_sem=total_sems.at[0], recv_sem=total_sems.at[1],
        device_id=(me, partner), device_id_type=MESH,
    )

    @pl.when(core == 0)
    def _():
        decay_link.start()
        for h in range(heads):
            chain_send[h] = state[h].astype(jnp.bfloat16)
            pair_link(h).start()

    pl.loop(0, groups)(add_earlier)

    @pl.when(core == 1)
    def _():
        decay_link.wait_recv()
        for h in range(heads):
            own_total = total[h : h + 1, :]
            both_total = own_total * pair_total[h : h + 1, :]
            pair_link(h).wait_recv()
            both_state = pair_recv[h].astype(jnp.float32) * own_total + state[h]

            @pl.when(chip > 0)
            def _():
                chip_link(h).wait_recv()

            @pl.when(chip < chips - 1)
            def _():
                before = chain_recv[h].astype(jnp.float32)
                chain_send[h] = (before * both_total + both_state).astype(jnp.bfloat16)
                chip_link(h).start()

            @pl.when(chip > 0)
            def _():
                relay_link(h).start()

        for h in range(heads):
            chain_used[h] = (
                chain_recv[h].astype(jnp.float32) * pair_total[h : h + 1, :]
                + pair_recv[h].astype(jnp.float32)
            ).astype(jnp.bfloat16)

    @pl.when(core == 0)
    def _():
        for h in range(heads):
            @pl.when(chip > 0)
            def _():
                relay_link(h).wait_recv()

            chain_used[h] = chain_recv[h]


    def finish(rank):
        head_cols = [slice(h * size, (h + 1) * size) for h in range(heads)]
        parts = [
            out_ref[rank, :, cols] + dot_nt(carry_ref[rank, :, cols], chain_used[h])
            for h, cols in enumerate(head_cols)
        ]
        for h, cols in enumerate(head_cols):
            back_send[rank, :, cols] = parts[h].astype(jnp.bfloat16)

    def leaving(rank):
        return pltpu.make_async_remote_copy(
            src_ref=back_send.at[rank], dst_ref=back_recv.at[rank],
            send_sem=back_send_sem.at[rank], recv_sem=back_recv_sem.at[rank],
            device_id=(peer_along(rank, -1), seq), device_id_type=MESH,
        )

    @pl.loop(1, groups)
    def _(rank):
        finish(rank)
        leaving(rank).start()

    finish(0)
    own_back = pltpu.make_async_copy(back_send.at[0], back_recv.at[0], back_recv_sem.at[0])
    own_back.start()
    out_weight_copy.wait()

    @pl.loop(0, groups // TOGETHER)
    def _(group):
        for n in range(TOGETHER):
            rank = group * TOGETHER + n
            pltpu.make_async_copy(
                back_send.at[rank], back_recv.at[rank], back_recv_sem.at[rank]
            ).wait()
            gathered[n * PIECE : (n + 1) * PIECE, :] = back_recv[rank]
        tile = 512
        for start in range(0, model_width, tile):
            cols = slice(start, start + tile)
            product = jnp.dot(
                gathered[...], out_weight_held[:, cols], preferred_element_type=jnp.float32
            ).astype(jnp.bfloat16)
            for n in range(TOGETHER):
                held[group * TOGETHER + n, :, cols] = product[n * PIECE : (n + 1) * PIECE]
        for n in range(TOGETHER):
            rank = group * TOGETHER + n
            pltpu.make_async_copy(held.at[rank], result.at[rank], result_sem.at[rank]).start()

    for rank in range(groups):
        pltpu.make_async_copy(held.at[rank], result.at[rank], result_sem.at[rank]).wait()
    @pl.loop(1, groups)
    def _(rank):
        arriving(rank).wait_send()
        leaving(rank).wait_send()

    @pl.when(core == 0)
    def _():
        decay_link.wait_send()
        for h in range(heads):
            pair_link(h).wait_send()

    @pl.when(core == 1)
    def _():
        for h in range(heads):
            @pl.when(chip < chips - 1)
            def _():
                chip_link(h).wait_send()

            @pl.when(chip > 0)
            def _():
                relay_link(h).wait_send()


def layer(
    source_dp, source_offset, doc_lengths, tokens, gain, weight, beta, bias, out_weight
):
    groups = source_dp.shape[0]
    rows, model_width = tokens.shape
    width = weight.shape[2]
    heads = beta.shape[1]
    size = width // heads
    smem = pl.BlockSpec(memory_space=pltpu.SMEM)
    vmem = pl.BlockSpec(memory_space=pltpu.VMEM)
    hbm = pl.BlockSpec(memory_space=pl.ANY)
    pieces = (groups, PIECE, model_width)
    narrow = (groups, PIECE, width)
    states = (heads, size, size)
    bfloat16, float32 = jnp.bfloat16, jnp.float32
    sems = pltpu.SemaphoreType.DMA((groups,))
    head_sems = pltpu.SemaphoreType.DMA((2, heads))
    sums = jnp.asarray(decay_sums(), bfloat16)
    return pl.pallas_call(
        layer_kernel,
        out_shape=(
            jax.ShapeDtypeStruct(pieces, bfloat16),
            jax.ShapeDtypeStruct((groups,), jnp.int32),
        ),
        in_specs=[smem] * 3 + [hbm, vmem, hbm, vmem, vmem, vmem, hbm],
        out_specs=(hbm, smem),
        scratch_shapes=[
            pltpu.SMEM((groups,), jnp.int32),
            pltpu.SMEM((groups,), jnp.int32),
            pltpu.SMEM((groups,), jnp.int32),
            pltpu.SMEM((doc_lengths.shape[0],), jnp.int32),
            pltpu.VMEM(pieces, bfloat16),
            pltpu.VMEM(pieces, bfloat16),
            pltpu.VMEM(pieces, bfloat16),
            pltpu.VMEM(weight.shape, bfloat16),
            pltpu.VMEM(out_weight.shape, bfloat16),
            pltpu.VMEM((TOGETHER * PIECE, model_width), bfloat16),
            pltpu.VMEM((3, TOGETHER, PIECE, width), bfloat16),
            pltpu.VMEM((TOGETHER, PIECE, heads), float32),
            pltpu.VMEM((2 * PIECE, width), bfloat16),
            pltpu.VMEM((4 * PIECE, width), float32),
            pltpu.VMEM((PIECE, width), bfloat16),
            pltpu.VMEM((5, PIECE, width), bfloat16),
            pltpu.VMEM(narrow, float32),
            pltpu.VMEM(narrow, bfloat16),
            pltpu.VMEM((groups,) + states, float32),
            pltpu.VMEM((groups, heads, size), float32),
            pltpu.VMEM(states, float32),
            pltpu.VMEM((heads, size), float32),
            pltpu.VMEM((groups,) + states, bfloat16),
            pltpu.VMEM((groups, heads, size), float32),
            pltpu.VMEM(states, bfloat16),
            pltpu.VMEM(states, bfloat16),
            pltpu.VMEM(states, bfloat16),
            pltpu.VMEM(states, bfloat16),
            pltpu.VMEM((heads, size), float32),
            pltpu.VMEM(narrow, bfloat16),
            pltpu.VMEM(narrow, bfloat16),
            pltpu.VMEM((TOGETHER * PIECE, width), bfloat16),
            pltpu.SemaphoreType.DMA,
            pltpu.SemaphoreType.DMA,
            pltpu.SemaphoreType.DMA,
            sems,
            sems,
            head_sems,
            head_sems,
            head_sems,
            pltpu.SemaphoreType.DMA((2,)),
            sems,
            sems,
            sems,
        ],
        compiler_params=pltpu.CompilerParams(
            collective_id=0, has_side_effects=True, vmem_limit_bytes=60 << 20
        ),
    )(
        source_dp, source_offset, doc_lengths, tokens.reshape(pieces), gain.reshape(1, -1), weight,
        beta.T, bias.reshape(1, -1), sums, out_weight,
    )


def place_kernel(rank_for, projected, result, held, in_sems, out_sems):
    pieces = projected.shape[0]
    arrive = [
        pltpu.make_async_copy(projected.at[jnp.clip(rank_for[n], 0, pieces - 1)], held.at[n], in_sems.at[n])
        for n in range(pieces)
    ]
    leave = [
        pltpu.make_async_copy(held.at[n], result.at[n], out_sems.at[n]) for n in range(pieces)
    ]
    for copy in arrive:
        copy.start()
    for n in range(pieces):
        arrive[n].wait()
        leave[n].start()
    for copy in leave:
        copy.wait()


def place_pieces(rank_for, projected):
    hbm = pl.BlockSpec(memory_space=pl.ANY)
    sems = pltpu.SemaphoreType.DMA((projected.shape[0],))
    return pl.pallas_call(
        place_kernel,
        out_shape=jax.ShapeDtypeStruct(projected.shape, projected.dtype),
        in_specs=[pl.BlockSpec(memory_space=pltpu.SMEM), hbm],
        out_specs=hbm,
        scratch_shapes=[pltpu.VMEM(projected.shape, projected.dtype), sems, sems],
    )(rank_for, projected)


def shards(
    tokens,
    norm_gain,
    qkv_weight,
    beta_weight,
    beta_bias,
    out_weight,
    doc_lengths,
    source_dp,
    source_offset,
):
    projected, rank_for = layer(
        source_dp, source_offset, doc_lengths.T, tokens, norm_gain, qkv_weight, beta_weight,
        beta_bias, out_weight,
    )
    return place_pieces(rank_for, projected).reshape(tokens.shape)


def solution(mesh):
    return jax.shard_map(
        shards,
        mesh=mesh,
        in_specs=(P(("dp", "seq"), None), P(), P(), P(), P(), P(), P(), P(), P()),
        out_specs=P(("dp", "seq"), None),
        check_vma=False,
    )
```
